32 devices in a mesh: section: 4 (over x, core), dp: 8 (over z, y).
Axes of the slice: x: 2, y: 2, z: 4, core: 2. Of those that a mesh axis runs over, the one named last changes fastest.
Arguments:
- stash: bfloat16 [4, 1024, 2048], P('section', 'dp'), may hold values from -6 to 6
- cotangent: bfloat16 [1024, 2048], P('dp', 'section'), may hold values from -6 to 6
- gate_weight: bfloat16 [4, 2048, 512], P('section', 'dp'), may hold values from -0.125 to 0.125
- up_weight: bfloat16 [4, 2048, 512], P('section', 'dp'), may hold values from -0.125 to 0.125
- down_weight: bfloat16 [4, 512, 2048], P('section'), may hold values from -0.25 to 0.25
- shared_gate: bfloat16 [4, 2048], P('section'), may hold values from -0.125 to 0.125
Outputs:
- grad_inputs: bfloat16 [4, 1024, 2048], P('section', 'dp')
- down_grad: float32 [4, 512, 2048], P('section', 'dp')
The draws below stay inside these ranges and needn't reach their ends.
All inputs are finite; a program needn't handle non-finite values.
Results may differ from the reference program's by a relative error of at most 0.029.
Values may be sent and summed in bfloat16 or wider, within the bound.
No kernel may reach another device: no remote copies, remote signals or barrier semaphores. Data moves between devices by JAX's collectives and lax.ppermute only.
A program may use at most 64 MiB of HBM per device.

```python
import jax
import jax.numpy as jnp
from jax import lax

D = 2048
FF = 512
LAYERS = 4
TOKENS = 1024
N_DP = 8


def steps_of(rng, extent, shards, low, largest):
    def one(dim, parts):
        draws = jax.random.uniform(jax.random.fold_in(jax.random.fold_in(rng, 6), dim), (parts,), jnp.float32, low / len(shards), largest / len(shards))
        return jnp.repeat(jnp.exp(draws), extent[dim] // parts).reshape((-1,) + (1,) * (len(extent) - dim - 1))

    gain = one(*shards[0])
    for cut in shards[1:]:
        gain = gain * one(*cut)
    return gain


def bell_draw(own_key, extent, spread, bound, pieces=(), kind=jnp.bfloat16):
    values = spread * jax.random.normal(own_key, extent, jnp.float32)
    if pieces:
        values = values * steps_of(own_key, extent, pieces, -0.22, 0.18)
    return jnp.clip(values, -bound, bound).astype(kind)


def setup_inputs(seed: int = 0) -> dict:
    arg_keys = jax.random.split(jax.random.key(seed), 7)
    stash = bell_draw(arg_keys[0], (LAYERS, TOKENS, D), 1.0, 6.0, ((0, 4), (1, 8)))
    cotangent = bell_draw(arg_keys[1], (TOKENS, D), 1.0, 6.0, ((0, 8), (1, 4)))
    gate_weight = bell_draw(arg_keys[2], (LAYERS, D, FF), D ** -0.5, 0.125, ((0, 4), (1, 8)))
    up_weight = bell_draw(arg_keys[3], (LAYERS, D, FF), D ** -0.5, 0.125, ((0, 4), (1, 8)))
    down_weight = bell_draw(arg_keys[4], (LAYERS, FF, D), FF ** -0.5, 0.25, ((0, 4),))
    shared_gate = bell_draw(arg_keys[5], (LAYERS, D), D ** -0.5, 0.125, ((0, 4),))
    return dict(stash=stash, cotangent=cotangent, gate_weight=gate_weight, up_weight=up_weight, down_weight=down_weight, shared_gate=shared_gate)


def backward_rows(inputs_now, grad_rows, joined, down_full, gate_vector):
    hidden_units = down_full.shape[0]
    projected = jnp.dot(inputs_now, joined, preferred_element_type=jnp.float32)
    gate_pre = projected[:, :hidden_units]
    up_pre = projected[:, hidden_units:]
    gate_score = jax.nn.sigmoid(jnp.dot(inputs_now, gate_vector, preferred_element_type=jnp.float32))[:, None]
    gate_sig = jax.nn.sigmoid(gate_pre)
    activated = gate_pre * gate_sig
    hidden = (activated * up_pre).astype(jnp.bfloat16)
    back_proj = lax.dot_general(grad_rows, down_full, (((1,), (1,)), ((), ())), preferred_element_type=jnp.float32)
    gate_sum = jnp.sum(back_proj * hidden.astype(jnp.float32), axis=1, keepdims=True)
    hidden_grad = gate_score * back_proj
    gate_grad = hidden_grad * up_pre * gate_sig * (1.0 + gate_pre * (1.0 - gate_sig))
    up_grad = hidden_grad * activated
    pair_grad = jnp.concatenate([gate_grad, up_grad], axis=1).astype(jnp.bfloat16)
    through = lax.dot_general(pair_grad, joined, (((1,), (1,)), ((), ())), preferred_element_type=jnp.float32)
    logit_grad = gate_sum * gate_score * (1.0 - gate_score)
    input_grad = (grad_rows.astype(jnp.float32) + through + logit_grad * gate_vector.astype(jnp.float32)[None, :]).astype(jnp.bfloat16)
    scaled = (gate_score * grad_rows.astype(jnp.float32)).astype(jnp.bfloat16)
    return input_grad, hidden, scaled


def replica_sum(group_pair):
    partial_sum = jnp.dot(group_pair[0].T, group_pair[1], preferred_element_type=jnp.float32).astype(jnp.bfloat16)
    return lax.optimization_barrier(partial_sum).astype(jnp.float32)


def reference(stash, cotangent, gate_weight, up_weight, down_weight, shared_gate):
    layer_count = stash.shape[0]
    grad_rows = cotangent
    input_grads = [None] * layer_count
    down_grads = [None] * layer_count
    for layer_index in range(layer_count - 1, -1, -1):
        joined = jnp.concatenate([gate_weight[layer_index], up_weight[layer_index]], axis=1)
        input_grad, hidden, scaled = backward_rows(stash[layer_count - 1 - layer_index], grad_rows, joined, down_weight[layer_index], shared_gate[layer_index])
        groups = (hidden.reshape(N_DP, -1, FF), scaled.reshape(N_DP, -1, D))
        partials = lax.map(replica_sum, groups)
        down_grads[layer_index] = jnp.sum(partials, axis=0) * (TOKENS ** -0.5)
        input_grads[layer_index] = input_grad
        grad_rows = input_grad
    return jnp.stack(input_grads), jnp.stack(down_grads)
```

```python
import jax
import jax.numpy as jnp
from jax import lax
from jax.sharding import PartitionSpec as P


def to_next(x, axis, pairs):
    return lax.ppermute(x, axis, pairs)


def ring_order(size):
    return [i for i in range(0, size, 2)] + [i for i in range(1, size, 2)][::-1]


def gather_ring(arrays, axis):
    size = lax.axis_size(axis)
    order = ring_order(size)
    ahead = [(order[i], order[(i + 1) % size]) for i in range(size)]
    back = [(b, a) for a, b in ahead]
    pieces = [list(arrays)]
    offsets = [0]
    from_back, from_ahead = list(arrays), list(arrays)
    for step in range(1, (size - 1) // 2 + 1):
        from_back = [to_next(v, axis, ahead) for v in from_back]
        from_ahead = [to_next(v, axis, back) for v in from_ahead]
        pieces += [from_back, from_ahead]
        offsets += [-step, step]
    if size % 2 == 0 and size > 1:
        half = len(arrays) // 2
        last = [
            to_next(v if i < half else w, axis, ahead if i < half else back)
            for i, (v, w) in enumerate(zip(from_back, from_ahead))
        ]
        pieces.append(last)
        offsets.append(size // 2)
    return pieces, offsets


def block_owner(offset, axis):
    size = lax.axis_size(axis)
    order = ring_order(size)
    place = [order.index(i) for i in range(size)]
    table = jnp.array([order[(place[i] + offset) % size] for i in range(size)], jnp.int32)
    return table[lax.axis_index(axis)]


def gather_to_last(x, axis):
    size = lax.axis_size(axis)
    width = 1
    while width < size:
        pairs = [(i, i + width) for i in range(width - 1, size - width, 2 * width)]
        x = jnp.concatenate([to_next(x, axis, pairs), x], axis=1)
        width *= 2
    return x


def reduce_rows(hidden, rows, axis):
    size = lax.axis_size(axis)
    inner = 2 if size % 2 == 0 else 1
    outer = size // inner
    me = lax.axis_index(axis)
    units = hidden.shape[1] // size
    width = rows.shape[1]
    cut = width * 11 // 16 // 128 * 128
    swap = [(i, i ^ 1) for i in range(size)]

    def turn(k):
        return [(i, (i + k * inner) % size) for i in range(size)]

    def block(k, j):
        place = (me // inner + k) % outer * inner + (me + j) % inner
        return lax.dynamic_slice_in_dim(hidden, place * units, units, 1)

    def product(blocks, columns):
        left = jnp.concatenate(blocks, axis=1)
        return lax.dot_general(
            left, columns, (((0,), (0,)), ((), ())), preferred_element_type=jnp.float32
        )

    first, second = rows[:, :cut], rows[:, cut:]
    send_a = product([block(k, 1) for k in range(outer)], first).astype(jnp.bfloat16)
    got_a = to_next(send_a, axis, swap)
    sums_b = product([block(0, j) for j in range(inner)], second)
    for k in range(1, outer):
        send = product([block(k, j) for j in range(inner)], second).astype(jnp.bfloat16)
        sums_b += to_next(send, axis, turn(k)).astype(jnp.float32)
    keep_a = product([block(k, 0) for k in range(outer)], first) + got_a.astype(jnp.float32)
    total_a = keep_a[:units]
    for k in range(1, outer):
        send = keep_a[k * units : (k + 1) * units].astype(jnp.bfloat16)
        total_a += to_next(send, axis, turn(k)).astype(jnp.float32)
    got_b = to_next(sums_b[units:].astype(jnp.bfloat16), axis, swap)
    total_b = sums_b[:units] + got_b.astype(jnp.float32)
    return jnp.concatenate([total_a, total_b], axis=1)


def on_device(stash, cotangent, gate_weight, up_weight, down_weight, shared_gate):
    sections = lax.axis_size("section")
    replicas = lax.axis_size("dp")
    section_index = lax.axis_index("section")
    local_rows = stash.shape[1]
    depth = gate_weight.shape[1]
    down_full = down_weight[0]
    gate_vector = shared_gate[0]
    hidden_units = down_full.shape[0]

    own_rows = to_next(stash[0], "section", [(i, sections - 1 - i) for i in range(sections)])
    seeded = gather_to_last(cotangent, "section")
    pieces, offsets = gather_ring([gate_weight[0], up_weight[0]], "dp")
    owners = [block_owner(offset, "dp") for offset in offsets]

    score = jax.nn.sigmoid(jnp.dot(own_rows, gate_vector, preferred_element_type=jnp.float32))[:, None]
    joined = jnp.zeros((depth * replicas, 2 * hidden_units), jnp.bfloat16)
    for owner, piece in zip(owners, pieces):
        joined = lax.dynamic_update_slice(
            joined, jnp.concatenate(piece, axis=1), (owner * depth, 0)
        )
    projected = jnp.dot(own_rows, joined, preferred_element_type=jnp.float32)
    gate_pre, up_pre = projected[:, :hidden_units], projected[:, hidden_units:]
    gate_sig = jax.nn.sigmoid(gate_pre)
    activated = gate_pre * gate_sig
    hidden = (activated * up_pre).astype(jnp.bfloat16)
    gate_scale = score * up_pre * gate_sig * (1.0 + gate_pre * (1.0 - gate_sig))
    up_scale = score * activated

    grad_rows = seeded
    results = grads = None
    for tick in range(sections):
        back_proj = lax.dot_general(
            grad_rows, down_full, (((1,), (1,)), ((), ())), preferred_element_type=jnp.float32
        )
        gate_sum = jnp.sum(back_proj * hidden.astype(jnp.float32), axis=1, keepdims=True)
        pair_grad = jnp.concatenate([back_proj * gate_scale, back_proj * up_scale], axis=1).astype(
            jnp.bfloat16
        )
        through = lax.dot_general(
            pair_grad, joined, (((1,), (1,)), ((), ())), preferred_element_type=jnp.float32
        )
        logit_grad = gate_sum * score * (1.0 - score)
        outgoing = (
            grad_rows.astype(jnp.float32)
            + through
            + logit_grad * gate_vector.astype(jnp.float32)[None, :]
        ).astype(jnp.bfloat16)
        here = section_index == sections - 1 - tick
        results = outgoing if tick == 0 else jnp.where(here, outgoing, results)
        grads = grad_rows if tick == 0 else jnp.where(here, grad_rows, grads)
        if tick < sections - 1:
            pairs = [(i, i - 1) for i in range(1, sections)]
            grad_rows = to_next(outgoing, "section", pairs)

    scaled = (score * grads.astype(jnp.float32)).astype(jnp.bfloat16)
    summed = reduce_rows(hidden, scaled, "dp")
    norm_factor = (local_rows * replicas) ** (-0.5)
    return (results[None], (summed * norm_factor)[None])


def solution(mesh):
    placed = (
        P("section", "dp", None),
        P("dp", "section"),
        P("section", "dp", None),
        P("section", "dp", None),
        P("section", None, None),
        P("section", None),
    )
    return jax.shard_map(
        on_device,
        mesh=mesh,
        in_specs=placed,
        out_specs=(P("section", "dp", None), P("section", "dp", None)),
        check_vma=False,
    )
```

```python
import functools

import jax
import jax.numpy as jnp
from jax import lax
from jax.experimental import pallas as pl
from jax.experimental.pallas import tpu as pltpu
from jax.sharding import PartitionSpec as P

F32, BF16 = jnp.float32, jnp.bfloat16
PLAIN = (((1,), (0,)), ((), ()))
TURNED = (((1,), (1,)), ((), ()))
VMEM = pl.BlockSpec(memory_space=pltpu.VMEM)
LIMIT = 16 * 2**20


def dot(left, right, dims):
    return lax.dot_general(left, right, dims, preferred_element_type=F32)


def params():
    return pltpu.CompilerParams(vmem_limit_bytes=LIMIT)


def cost(macs, *arrays):
    moved = sum(a.size * a.dtype.itemsize for a in arrays)
    return pl.CostEstimate(flops=2 * macs, bytes_accessed=moved, transcendentals=0)


def ring_place(index, size):
    return jnp.where(index % 2 == 0, index // 2, size - 1 - index // 2)


def ring_member(place, size):
    return jnp.where(place < (size + 1) // 2, 2 * place, 2 * (size - 1 - place) + 1)


def ring_pairs(size):
    order = list(range(0, size, 2)) + list(range(1, size, 2))[::-1]
    ahead = [(order[i], order[(i + 1) % size]) for i in range(size)]
    return ahead, [(b, a) for a, b in ahead]


def gather_ring(arrays, axis):
    size = lax.axis_size(axis)
    ahead, back = ring_pairs(size)
    pieces, offsets = [list(arrays)], [0]
    from_back, from_ahead = list(arrays), list(arrays)
    for step in range(1, (size - 1) // 2 + 1):
        from_back = [lax.ppermute(v, axis, ahead) for v in from_back]
        from_ahead = [lax.ppermute(v, axis, back) for v in from_ahead]
        pieces += [from_back, from_ahead]
        offsets += [-step, step]
    if size % 2 == 0:
        pieces.append(
            [lax.ppermute(from_back[0], axis, ahead), lax.ppermute(from_ahead[1], axis, back)]
        )
        offsets.append(size // 2)
    return pieces, offsets


def gather_to_ends(x, axis):
    size = lax.axis_size(axis)
    steps = [1 << place for place in range(size.bit_length() - 1)]
    needed = [{0, size - 1}]
    for stride in steps[::-1]:
        needed.append(needed[-1] | {i ^ stride for i in needed[-1]})
    held = [x]
    for stride, wanted in zip(steps, needed[-2::-1]):
        pairs = [(i ^ stride, i) for i in sorted(wanted)]
        held = held + [lax.ppermute(v, axis, pairs) for v in held]
    return held


def after(values, *others):
    return lax.optimization_barrier((values, others))[0]


def piece_columns(offset, axis, depth):
    if offset is None:
        return slice(0, depth)
    size = lax.axis_size(axis)
    place = (ring_place(lax.axis_index(axis), size) + (offset + size)) % size
    return pl.ds(pl.multiple_of(ring_member(place, size) * depth, depth), depth)


def push_back(grad_ref, back_proj, scales, gate_vector, pieces, columns, out_ref):
    gate_scale, up_scale, logit_scale = scales
    logit = jnp.sum(back_proj * logit_scale[...], axis=1, keepdims=True)
    gate_grad = (back_proj * gate_scale[...]).astype(BF16)
    up_grad = (back_proj * up_scale[...]).astype(BF16)
    for where, (gate, up) in zip(columns, pieces):
        through = dot(gate_grad, gate[...], TURNED) + dot(up_grad, up[...], TURNED)
        out_ref[:, where] = (
            grad_ref[:, where].astype(F32) + through + logit * gate_vector[:, where].astype(F32)
        ).astype(BF16)


def pair_up(refs):
    return [refs[i : i + 2] for i in range(0, len(refs), 2)]


def prepare_kernel(rows, gate_vector, down, *rest):
    blocks, (seeded, score, back_proj) = rest[:-3], rest[-3:]
    sections = lax.axis_size("section")
    is_last = lax.axis_index("section") == sections - 1
    width = blocks[0].shape[1]

    def lay(order):
        for place, block in enumerate(order):
            seeded[:, place * width : (place + 1) * width] = block[...]

    pl.when(is_last)(lambda: lay(blocks[::-1]))
    pl.when(jnp.logical_not(is_last))(lambda: lay(blocks))
    logit = jnp.sum(
        rows[...].astype(F32) * gate_vector[...].astype(F32), axis=1, keepdims=True
    )
    score[...] = jax.nn.sigmoid(logit)
    back_proj[...] = dot(seeded[...], down[...], TURNED)


def first_kernel(offsets, rows, score, back_proj, grad, gate_vector, *rest):
    pieces = pair_up(rest[: 2 * len(offsets)])
    out, gate_scale, up_scale, logit_scale, scored = rest[2 * len(offsets) :]
    depth = pieces[0][0].shape[0]
    columns = [piece_columns(offset, "dp", depth) for offset in offsets]
    gate_pre = up_pre = 0.0
    for where, (gate, up) in zip(columns, pieces):
        block = rows[:, where]
        gate_pre += dot(block, gate[...], PLAIN)
        up_pre += dot(block, up[...], PLAIN)
    gate_sig = jax.nn.sigmoid(gate_pre)
    activated = gate_pre * gate_sig
    hidden = (activated * up_pre).astype(BF16).astype(F32)
    share = score[...]
    gate_scale[...] = share * up_pre * gate_sig * (1.0 + gate_pre * (1.0 - gate_sig))
    up_scale[...] = share * activated
    logit_scale[...] = hidden * (share * (1.0 - share))
    scored[...] = (hidden * share).astype(BF16)
    scales = gate_scale, up_scale, logit_scale
    push_back(grad, back_proj[...], scales, gate_vector, pieces, columns, out)


def tick_kernel(offsets, section, grad, held, down, gate_vector, a, b, c, *rest):
    pieces, out = pair_up(rest[:-1]), rest[-1]

    here = lax.axis_index("section") == section

    @pl.when(jnp.logical_not(here))
    def _():
        out[...] = held[...]

    @pl.when(here)
    def _():
        depth = pieces[0][0].shape[0]
        columns = [piece_columns(offset, "dp", depth) for offset in offsets]
        back_proj = dot(grad[...], down[...], TURNED)
        push_back(grad, back_proj, (a, b, c), gate_vector, pieces, columns, out)


def products_kernel(inner, cut, scored, grad, first_grad, keep_a, keep_b, send_a, *rest):
    send_b, turned = rest[:-1], rest[-1]
    size = lax.axis_size("dp")
    outer = size // inner
    units = scored.shape[1] // size
    me = lax.axis_index("dp")
    turned[...] = scored[...].T

    def block(k, j):
        place = (me // inner + k) % outer * inner + (me + j) % inner
        return turned[pl.ds(pl.multiple_of(place * units, units), units), :]

    def work(source):
        for k in range(outer):
            rows = slice(k * units, (k + 1) * units)
            send_a[rows, :] = dot(block(k, 1), source[:, :cut], PLAIN).astype(BF16)
            keep_a[rows, :] = dot(block(k, 0), source[:, :cut], PLAIN)
            for j in range(inner):
                rows = slice(j * units, (j + 1) * units)
                found = dot(block(k, j), source[:, cut:], PLAIN)
                if k == 0:
                    keep_b[rows, :] = found
                else:
                    send_b[k - 1][rows, :] = found.astype(BF16)

    is_first = lax.axis_index("section") == 0
    pl.when(is_first)(lambda: work(first_grad))
    pl.when(jnp.logical_not(is_first))(lambda: work(grad))


def reduce_rows(scored, grad, first_grad, axis):
    size = lax.axis_size(axis)
    inner = 2
    outer = size // inner
    tokens, hidden_units = scored.shape
    units = hidden_units // size
    width = grad.shape[1]
    cut = width * 11 // 16 // 128 * 128
    swap = [(i, i ^ 1) for i in range(size)]

    def turn(k):
        return [(i, (i + k * inner) % size) for i in range(size)]

    shape = jax.ShapeDtypeStruct
    keep_a, sum_b, send_a, *send_b = pl.pallas_call(
        functools.partial(products_kernel, inner, cut),
        out_shape=[
            shape((outer * units, cut), F32),
            shape((inner * units, width - cut), F32),
            shape((outer * units, cut), BF16),
        ]
        + [shape((inner * units, width - cut), BF16)] * (outer - 1),
        in_specs=[VMEM] * 3,
        out_specs=[VMEM] * (outer + 2),
        scratch_shapes=[pltpu.VMEM((hidden_units, tokens), BF16)],
        compiler_params=params(),
        cost_estimate=cost(tokens * hidden_units * width, scored, grad),
        name="products",
    )(scored, grad, first_grad)
    sum_a = keep_a + lax.ppermute(send_a, axis, swap).astype(F32)
    for k in range(1, outer):
        sum_b += lax.ppermute(send_b[k - 1], axis, turn(k)).astype(F32)
    total_a = sum_a[:units]
    for k in range(1, outer):
        send = sum_a[k * units : (k + 1) * units].astype(BF16)
        total_a += lax.ppermute(send, axis, turn(k)).astype(F32)
    got_b = lax.ppermute(sum_b[units:].astype(BF16), axis, swap)
    total_b = sum_b[:units] + got_b.astype(F32)
    return jnp.concatenate([total_a, total_b], axis=1)


def on_device(stash, cotangent, gate_weight, up_weight, down_weight, shared_gate):
    sections = lax.axis_size("section")
    replicas = lax.axis_size("dp")
    local_rows, model_width = stash.shape[1:]
    depth = gate_weight.shape[1]
    down_full = down_weight[0]
    hidden_units = down_full.shape[0]

    pieces, offsets = gather_ring([gate_weight[0], up_weight[0]], "dp")
    stash, cotangent = after((stash, cotangent), pieces[min(1, len(pieces) - 1)])
    own_rows = lax.ppermute(stash[0], "section", [(i, sections - 1 - i) for i in range(sections)])
    blocks = gather_to_ends(cotangent, "section")
    shape = jax.ShapeDtypeStruct
    small = shape((local_rows, hidden_units), F32)
    seeded, score, back_proj = pl.pallas_call(
        prepare_kernel,
        out_shape=[shape((local_rows, model_width), BF16), shape((local_rows, 1), F32), small],
        in_specs=[VMEM] * (3 + len(blocks)),
        out_specs=[VMEM] * 3,
        compiler_params=params(),
        cost_estimate=cost(local_rows * model_width * hidden_units, down_full, own_rows),
        name="prepare",
    )(own_rows, shared_gate, down_full, *blocks)

    if depth % 128:
        size = replicas
        place = ring_place(lax.axis_index("dp"), size)
        joined = [jnp.zeros((depth * replicas, hidden_units), BF16)] * 2
        for offset, piece in zip(offsets, pieces):
            start = ring_member((place + offset + size) % size, size) * depth
            joined = [lax.dynamic_update_slice(j, p, (start, 0)) for j, p in zip(joined, piece)]
        pieces, offsets = [joined], [None]
    flat = [v for piece in pieces for v in piece]

    outgoing, *scales, scored = pl.pallas_call(
        functools.partial(first_kernel, offsets),
        out_shape=[
            shape((local_rows, model_width), BF16),
            small,
            small,
            small,
            shape((local_rows, hidden_units), BF16),
        ],
        in_specs=[VMEM] * (5 + len(flat)),
        out_specs=[VMEM] * 5,
        compiler_params=params(),
        cost_estimate=cost(4 * local_rows * model_width * hidden_units, *flat),
        name="first_tick",
    )(own_rows, score, back_proj, seeded, shared_gate, *flat)
    scored = lax.ppermute(scored, "section", [(i, (i + 1) % sections) for i in range(sections)])

    def tick(section, grad, held):
        return pl.pallas_call(
            functools.partial(tick_kernel, offsets, section),
            out_shape=shape((local_rows, model_width), BF16),
            in_specs=[VMEM] * (7 + len(flat)),
            out_specs=VMEM,
            compiler_params=params(),
            cost_estimate=cost(3 * local_rows * model_width * hidden_units, *flat),
            name="tick",
        )(grad, held, down_full, shared_gate, *scales, *flat)

    for section in range(sections - 2, -1, -1):
        if section == 0:
            summed = reduce_rows(scored, outgoing, seeded, "dp")
        grad = lax.ppermute(outgoing, "section", [(section + 1, section)])
        outgoing = tick(section, grad, outgoing)

    summed = lax.ppermute(
        summed.astype(BF16), "section", [(i, (i - 1) % sections) for i in range(sections)]
    ).astype(F32)
    norm_factor = (local_rows * replicas) ** (-0.5)
    return (outgoing[None], (summed * norm_factor)[None])


def solution(mesh):
    placed = (
        P("section", "dp", None),
        P("dp", "section"),
        P("section", "dp", None),
        P("section", "dp", None),
        P("section", None, None),
        P("section", None),
    )
    return jax.shard_map(
        on_device,
        mesh=mesh,
        in_specs=placed,
        out_specs=(P("section", "dp", None), P("section", "dp", None)),
        check_vma=False,
    )
```

```python
import functools

import jax
import jax.numpy as jnp
from jax import lax
from jax.experimental import pallas as pl
from jax.experimental.pallas import tpu as pltpu
from jax.sharding import PartitionSpec as P

F32, BF16 = jnp.float32, jnp.bfloat16
PLAIN = (((1,), (0,)), ((), ()))
TURNED = (((1,), (1,)), ((), ()))
VMEM = pl.BlockSpec(memory_space=pltpu.VMEM)
LIMIT = 16 * 2**20


def dot(left, right, dims):
    return lax.dot_general(left, right, dims, preferred_element_type=F32)


def params():
    return pltpu.CompilerParams(vmem_limit_bytes=LIMIT)


def cost(macs, *arrays):
    moved = sum(a.size * a.dtype.itemsize for a in arrays)
    return pl.CostEstimate(flops=2 * macs, bytes_accessed=moved, transcendentals=0)


def ring_place(index, size):
    return jnp.where(index % 2 == 0, index // 2, size - 1 - index // 2)


def ring_member(place, size):
    return jnp.where(place < (size + 1) // 2, 2 * place, 2 * (size - 1 - place) + 1)


def ring_pairs(size):
    order = list(range(0, size, 2)) + list(range(1, size, 2))[::-1]
    ahead = [(order[i], order[(i + 1) % size]) for i in range(size)]
    return ahead, [(b, a) for a, b in ahead]


def gather_ring(arrays, axis, between):
    size = lax.axis_size(axis)
    ahead, back = ring_pairs(size)
    pieces, offsets = [list(arrays)], [0]
    moving = [(v, v) for v in arrays]
    for step in range(1, (size - 1) // 2 + 1):
        moved = []
        for i, (v, w) in enumerate(moving):
            v, w = between(step, i, (v, w))
            both = lax.ppermute(v, axis, ahead), lax.ppermute(w, axis, back)
            moved.append(lax.optimization_barrier(both))
        moving = moved
        pieces += [[v for v, _ in moving], [w for _, w in moving]]
        offsets += [-step, step]
    if size % 2 == 0:
        (v, _), (_, w) = between(size // 2, 0, moving[0]), between(size // 2, 1, moving[1])
        pieces.append([lax.ppermute(v, axis, ahead), lax.ppermute(w, axis, back)])
        offsets.append(size // 2)
    return pieces, offsets


def gather_to_ends(x, axis):
    size = lax.axis_size(axis)
    steps = [1 << place for place in range(size.bit_length() - 1)][::-1]
    needed = [{0, size - 1}]
    for stride in steps[::-1]:
        needed.append(needed[-1] | {i ^ stride for i in needed[-1]})
    held, offsets = [x], [0]
    yield held, offsets
    for stride, wanted in zip(steps, needed[-2::-1]):
        pairs = [(i ^ stride, i) for i in sorted(wanted)]
        held += [lax.ppermute(block, axis, pairs) for block in list(held)]
        offsets += [offset ^ stride for offset in offsets]
        yield held, offsets


def after(values, *others):
    return lax.optimization_barrier((values, others))[0]


def piece_columns(offset, axis, depth):
    if offset is None:
        return slice(0, depth)
    size = lax.axis_size(axis)
    place = (ring_place(lax.axis_index(axis), size) + (offset + size)) % size
    return pl.ds(pl.multiple_of(ring_member(place, size) * depth, depth), depth)


def push_back(grad_ref, back_proj, scales, gate_vector, pieces, columns, out_ref):
    gate_scale, up_scale, logit_scale = scales
    logit = jnp.sum(back_proj * logit_scale[...], axis=1, keepdims=True)
    gate_grad = (back_proj * gate_scale[...]).astype(BF16)
    up_grad = (back_proj * up_scale[...]).astype(BF16)
    for where, (gate, up) in zip(columns, pieces):
        through = dot(gate_grad, gate[...], TURNED) + dot(up_grad, up[...], TURNED)
        out_ref[:, where] = (
            grad_ref[:, where].astype(F32) + through + logit * gate_vector[:, where].astype(F32)
        ).astype(BF16)


def pair_up(refs):
    return [refs[i : i + 2] for i in range(0, len(refs), 2)]


def score_kernel(rows, gate_vector, score):
    logit = jnp.sum(
        rows[...].astype(F32) * gate_vector[...].astype(F32), axis=1, keepdims=True
    )
    score[...] = jax.nn.sigmoid(logit)


def prepare_kernel(offsets, down, *rest):
    blocks, (seeded, back_proj) = rest[:-2], rest[-2:]
    sections = lax.axis_size("section")
    is_last = lax.axis_index("section") == sections - 1
    width = blocks[0].shape[1]

    def lay(flip):
        for offset, block in zip(offsets, blocks):
            place = offset ^ flip
            seeded[:, place * width : (place + 1) * width] = block[...]

    pl.when(is_last)(lambda: lay(sections - 1))
    pl.when(jnp.logical_not(is_last))(lambda: lay(0))
    back_proj[...] = dot(seeded[...], down[...], TURNED)


def first_kernel(offsets, rows, score, back_proj, grad, gate_vector, *rest):
    pieces = pair_up(rest[: 2 * len(offsets)])
    out, gate_scale, up_scale, logit_scale, scored = rest[2 * len(offsets) :]
    depth = pieces[0][0].shape[0]
    columns = [piece_columns(offset, "dp", depth) for offset in offsets]
    gate_pre = up_pre = 0.0
    for where, (gate, up) in zip(columns, pieces):
        block = rows[:, where]
        gate_pre += dot(block, gate[...], PLAIN)
        up_pre += dot(block, up[...], PLAIN)
    gate_sig = jax.nn.sigmoid(gate_pre)
    activated = gate_pre * gate_sig
    hidden = (activated * up_pre).astype(BF16).astype(F32)
    share = score[...]
    gate_scale[...] = share * up_pre * gate_sig * (1.0 + gate_pre * (1.0 - gate_sig))
    up_scale[...] = share * activated
    logit_scale[...] = hidden * (share * (1.0 - share))
    scored[...] = (hidden * share).astype(BF16).T
    scales = gate_scale, up_scale, logit_scale
    section, sections = lax.axis_index("section"), lax.axis_size("section")

    @pl.when(section == sections - 1)
    def _():
        push_back(grad, back_proj[...], scales, gate_vector, pieces, columns, out)

    @pl.when(section < sections - 1)
    def _():
        out[...] = grad[...]


def tick_kernel(offsets, section, grad, held, down, gate_vector, a, b, c, *rest):
    pieces, out = pair_up(rest[:-1]), rest[-1]

    here = lax.axis_index("section") == section

    @pl.when(jnp.logical_not(here))
    def _():
        out[...] = held[...]

    @pl.when(here)
    def _():
        depth = pieces[0][0].shape[0]
        columns = [piece_columns(offset, "dp", depth) for offset in offsets]
        back_proj = dot(grad[...], down[...], TURNED)
        push_back(grad, back_proj, (a, b, c), gate_vector, pieces, columns, out)


def block_rows(bits, rest, units):
    return pl.ds(pl.multiple_of((rest * 4 + 2 * bits[1] + bits[0]) * units, units), units)


def own_bits():
    me = lax.axis_index("dp")
    return me % 2, me // 2 % 2


def split_kernel(scored, *out):
    size = lax.axis_size("dp")
    units = scored.shape[0] // size
    own = own_bits()
    for bit in range(2):
        for second in range(2):
            for rest in range(size // 4):
                bits = (1 - own[0], second) if bit == 0 else (second, 1 - own[1])
                start = (second * (size // 4) + rest) * units
                out[bit][start : start + units, :] = scored[block_rows(bits, rest, units), :]


def products_kernel(scored, grad, *rest):
    theirs, partners, sends, keeps = rest[:2], rest[2:4], rest[4:6], rest[6:]
    size = lax.axis_size("dp")
    units = scored.shape[0] // size
    half, width = sends[0].shape
    own = own_bits()
    for bit in range(2):
        columns = slice(bit * width, (bit + 1) * width)
        mine = grad[:, columns]

        def rows(second):
            bits = (own[0], second) if bit == 0 else (second, own[1])
            blocks = [scored[block_rows(bits, rest, units), :] for rest in range(size // 4)]
            where = pl.ds(pl.multiple_of(second * half, half), half)
            left = jnp.concatenate(blocks, axis=0)
            return dot(left, mine, PLAIN) + dot(theirs[bit][where, :], partners[bit][...], PLAIN)

        sends[bit][...] = rows(1 - own[1 - bit]).astype(BF16)
        keeps[bit][...] = rows(own[1 - bit])


def combine_kernel(bit, count, *refs):
    keeps, gots, outs = refs[:count], refs[count : 2 * count], refs[2 * count :]
    width = keeps[0].shape[1]
    for i, (keep, got) in enumerate(zip(keeps, gots)):
        columns = slice(i * width, (i + 1) * width)
        if bit is None:
            outs[0][:, columns] = (keep[...] + got[...].astype(F32)).astype(BF16)
            continue
        half = keep.shape[0] // 2
        own = lax.axis_index("dp") >> bit & 1

        def rows(which):
            where = pl.ds(pl.multiple_of(which * half, half), half)
            return keep[where, :] + got[where, :].astype(F32)

        outs[0][:, columns] = rows(1 - own).astype(BF16)
        outs[1][:, columns] = rows(own)


def along(bit, *values):
    pairs = [(i, i ^ 1 << bit) for i in range(lax.axis_size("dp"))]
    return [lax.ppermute(v, "dp", pairs) for v in values]


def call(kernel, name, outs, macs, *args):
    return pl.pallas_call(
        kernel,
        out_shape=outs,
        in_specs=[VMEM] * len(args),
        out_specs=[VMEM] * len(outs),
        compiler_params=params(),
        cost_estimate=cost(macs, *args),
        name=name,
    )(*args)


def swap_scored(scored):
    half = jax.ShapeDtypeStruct((scored.shape[0] // 2, scored.shape[1]), BF16)
    to_first, to_second = call(split_kernel, "split", [half] * 2, 0, scored)
    return [*along(0, to_first), *along(1, to_second)]


def reduce_rows(scored, theirs, grad):
    size = lax.axis_size("dp")
    rows, width = scored.shape[0] // 4, grad.shape[1]
    shape = jax.ShapeDtypeStruct
    partners = [*along(0, grad[:, : width // 2]), *along(1, grad[:, width // 2 :])]
    half = (rows, width // 2)
    outs = [shape(half, BF16)] * 2 + [shape(half, F32)] * 2
    macs = 4 * rows * scored.shape[1] * width
    *sends, keep_a, keep_b = call(
        products_kernel, "products", outs, macs, scored, grad, *theirs, *partners
    )
    keeps = [keep_a, keep_b]
    gots = [*along(1, sends[0]), *along(0, sends[1])]
    for bit in range(size.bit_length() - 2, 1, -1):
        rows //= 2
        outs = [shape((rows, width), BF16), shape((rows, width), F32)]
        kernel = functools.partial(combine_kernel, bit, len(keeps))
        send, keep = call(kernel, "combine", outs, 0, *keeps, *gots)
        keeps, gots = [keep], along(bit, send)
    kernel = functools.partial(combine_kernel, None, len(keeps))
    return call(kernel, "total", [shape((rows, width), BF16)], 0, *keeps, *gots)[0]


def on_device(stash, cotangent, gate_weight, up_weight, down_weight, shared_gate):
    sections = lax.axis_size("section")
    replicas = lax.axis_size("dp")
    local_rows, model_width = stash.shape[1:]
    depth = gate_weight.shape[1]
    down_full = down_weight[0]
    hidden_units = down_full.shape[0]

    shape = jax.ShapeDtypeStruct
    small = shape((local_rows, hidden_units), F32)
    cotangents = gather_to_ends(cotangent, "section")
    blocks, block_offsets = next(cotangents)
    own_rows = stash[0]

    def between(step, i, moving):
        nonlocal blocks, own_rows
        if step == 1 and i == 1:
            blocks, _ = next(cotangents, (blocks, None))
        if step == 2 and i == 0:
            own_rows, *moving = after((own_rows, *moving))
            mirrored = [(k, sections - 1 - k) for k in range(sections)]
            own_rows = lax.ppermute(own_rows, "section", mirrored)
        if step == 2 and i == 1:
            moving, blocks = after((moving, blocks))
            blocks, _ = next(cotangents, (list(blocks), None))
        if step == 3 and i == 1:
            moving, blocks = after((moving, blocks))
        if step == replicas // 2 and i == 0:
            moving, own_rows = after((moving, own_rows))
        return moving

    pieces, offsets = gather_ring([gate_weight[0], up_weight[0]], "dp", between)
    for blocks, _ in cotangents:
        pass
    seeded, back_proj = pl.pallas_call(
        functools.partial(prepare_kernel, block_offsets),
        out_shape=[shape((local_rows, model_width), BF16), small],
        in_specs=[VMEM] * (1 + len(blocks)),
        out_specs=[VMEM] * 2,
        compiler_params=params(),
        cost_estimate=cost(local_rows * model_width * hidden_units, down_full),
        name="prepare",
    )(down_full, *blocks)
    score = pl.pallas_call(
        score_kernel,
        out_shape=shape((local_rows, 1), F32),
        in_specs=[VMEM] * 2,
        out_specs=VMEM,
        compiler_params=params(),
        cost_estimate=cost(local_rows * model_width, own_rows),
        name="score",
    )(own_rows, shared_gate)

    if depth % 128:
        size = replicas
        place = ring_place(lax.axis_index("dp"), size)
        joined = [jnp.zeros((depth * replicas, hidden_units), BF16)] * 2
        for offset, piece in zip(offsets, pieces):
            start = ring_member((place + offset + size) % size, size) * depth
            joined = [lax.dynamic_update_slice(j, p, (start, 0)) for j, p in zip(joined, piece)]
        pieces, offsets = [joined], [None]
    flat = [v for piece in pieces for v in piece]

    outgoing, *scales, scored = pl.pallas_call(
        functools.partial(first_kernel, offsets),
        out_shape=[
            shape((local_rows, model_width), BF16),
            small,
            small,
            small,
            shape((hidden_units, local_rows), BF16),
        ],
        in_specs=[VMEM] * (5 + len(flat)),
        out_specs=[VMEM] * 5,
        compiler_params=params(),
        cost_estimate=cost(4 * local_rows * model_width * hidden_units, *flat),
        name="first_tick",
    )(own_rows, score, back_proj, seeded, shared_gate, *flat)
    around = [(i, (i + 1) % sections) for i in range(sections)]
    scored = lax.ppermute(scored, "section", around)

    def tick(section, grad, held):
        return pl.pallas_call(
            functools.partial(tick_kernel, offsets, section),
            out_shape=shape((local_rows, model_width), BF16),
            in_specs=[VMEM] * (7 + len(flat)),
            out_specs=VMEM,
            compiler_params=params(),
            cost_estimate=cost(3 * local_rows * model_width * hidden_units, *flat),
            name="tick",
        )(grad, held, down_full, shared_gate, *scales, *flat)

    for section in range(sections - 2, -1, -1):
        if section == 0:
            reduced = reduce_rows(scored, theirs, outgoing)
        if section == sections - 3:
            outgoing, scored = after((outgoing, scored))
        grad = lax.ppermute(outgoing, "section", [(section + 1, section)])
        if section == max(sections - 3, 0):
            theirs = swap_scored(scored)
        outgoing = tick(section, grad, outgoing)

    reduced = lax.ppermute(reduced, "section", [(b, a) for a, b in around])
    norm_factor = (local_rows * replicas) ** (-0.5)
    return (outgoing[None], (reduced.astype(F32) * norm_factor)[None])


def solution(mesh):
    placed = (
        P("section", "dp", None),
        P("dp", "section"),
        P("section", "dp", None),
        P("section", "dp", None),
        P("section", None, None),
        P("section", None),
    )
    return jax.shard_map(
        on_device,
        mesh=mesh,
        in_specs=placed,
        out_specs=(P("section", "dp", None), P("section", "dp", None)),
        check_vma=False,
    )
```

```python
import functools

import jax
import jax.numpy as jnp
from jax import lax
from jax.experimental import pallas as pl
from jax.experimental.pallas import tpu as pltpu
from jax.sharding import PartitionSpec as P

F32, BF16 = jnp.float32, jnp.bfloat16
PLAIN = (((1,), (0,)), ((), ()))
TURNED = (((1,), (1,)), ((), ()))
VMEM = pl.BlockSpec(memory_space=pltpu.VMEM)
LIMIT = 16 * 2**20


def dot(left, right, dims):
    return lax.dot_general(left, right, dims, preferred_element_type=F32)


def params():
    return pltpu.CompilerParams(vmem_limit_bytes=LIMIT)


def cost(macs, *arrays):
    moved = sum(a.size * a.dtype.itemsize for a in arrays)
    return pl.CostEstimate(flops=2 * macs, bytes_accessed=moved, transcendentals=0)


def ring_place(index, size):
    return jnp.where(index % 2 == 0, index // 2, size - 1 - index // 2)


def ring_member(place, size):
    return jnp.where(place < (size + 1) // 2, 2 * place, 2 * (size - 1 - place) + 1)


def ring_pairs(size):
    order = list(range(0, size, 2)) + list(range(1, size, 2))[::-1]
    ahead = [(order[i], order[(i + 1) % size]) for i in range(size)]
    return ahead, [(b, a) for a, b in ahead]


def gather_ring(arrays, axis, between):
    size = lax.axis_size(axis)
    ahead, back = ring_pairs(size)
    pieces, offsets = [list(arrays)], [0]
    moving = [(v, v) for v in arrays]
    for step in range(1, (size - 1) // 2 + 1):
        moved = []
        for i, (v, w) in enumerate(moving):
            v, w = between(step, i, (v, w))
            both = lax.ppermute(v, axis, ahead), lax.ppermute(w, axis, back)
            moved.append(lax.optimization_barrier(both))
        moving = moved
        pieces += [[v for v, _ in moving], [w for _, w in moving]]
        offsets += [-step, step]
    if size % 2 == 0:
        (v, _), (_, w) = between(size // 2, 0, moving[0]), between(size // 2, 1, moving[1])
        pieces.append([lax.ppermute(v, axis, ahead), lax.ppermute(w, axis, back)])
        offsets.append(size // 2)
    return pieces, offsets


def gather_to_ends(x, axis):
    size = lax.axis_size(axis)
    steps = [1 << place for place in range(size.bit_length() - 1)][::-1]
    needed = [{0, size - 1}]
    for stride in steps[::-1]:
        needed.append(needed[-1] | {i ^ stride for i in needed[-1]})
    held, offsets = [x], [0]
    yield held, offsets
    for stride, wanted in zip(steps, needed[-2::-1]):
        pairs = [(i ^ stride, i) for i in sorted(wanted)]
        held += [lax.ppermute(block, axis, pairs) for block in list(held)]
        offsets += [offset ^ stride for offset in offsets]
        yield held, offsets


def after(values, *others):
    return lax.optimization_barrier((values, others))[0]


def piece_columns(offset, axis, depth):
    if offset is None:
        return slice(0, depth)
    size = lax.axis_size(axis)
    place = (ring_place(lax.axis_index(axis), size) + (offset + size)) % size
    return pl.ds(pl.multiple_of(ring_member(place, size) * depth, depth), depth)


def push_back(grad_ref, back_proj, scales, gate_vector, pieces, columns, out_ref):
    gate_scale, up_scale, logit_scale = scales
    logit = jnp.sum(back_proj * logit_scale[...], axis=1, keepdims=True)
    gate_grad = (back_proj * gate_scale[...]).astype(BF16)
    up_grad = (back_proj * up_scale[...]).astype(BF16)
    for where, (gate, up) in zip(columns, pieces):
        through = dot(gate_grad, gate[...], TURNED) + dot(up_grad, up[...], TURNED)
        out_ref[:, where] = (
            grad_ref[:, where].astype(F32) + through + logit * gate_vector[:, where].astype(F32)
        ).astype(BF16)


def pair_up(refs):
    return [refs[i : i + 2] for i in range(0, len(refs), 2)]


def score_kernel(rows, gate_vector, score):
    logit = jnp.sum(
        rows[...].astype(F32) * gate_vector[...].astype(F32), axis=1, keepdims=True
    )
    score[...] = jax.nn.sigmoid(logit)


def prepare_kernel(offsets, down, *rest):
    blocks, (seeded, back_proj) = rest[:-2], rest[-2:]
    sections = lax.axis_size("section")
    is_last = lax.axis_index("section") == sections - 1
    width = blocks[0].shape[1]

    def lay(flip):
        for offset, block in zip(offsets, blocks):
            place = offset ^ flip
            seeded[:, place * width : (place + 1) * width] = block[...]

    pl.when(is_last)(lambda: lay(sections - 1))
    pl.when(jnp.logical_not(is_last))(lambda: lay(0))
    back_proj[...] = dot(seeded[...], down[...], TURNED)


def first_kernel(offsets, rows, score, back_proj, grad, gate_vector, *rest):
    pieces = pair_up(rest[: 2 * len(offsets)])
    out, gate_scale, up_scale, logit_scale, scored = rest[2 * len(offsets) :]
    depth = pieces[0][0].shape[0]
    columns = [piece_columns(offset, "dp", depth) for offset in offsets]
    gate_pre = up_pre = 0.0
    for where, (gate, up) in zip(columns, pieces):
        block = rows[:, where]
        gate_pre += dot(block, gate[...], PLAIN)
        up_pre += dot(block, up[...], PLAIN)
    gate_sig = jax.nn.sigmoid(gate_pre)
    activated = gate_pre * gate_sig
    hidden = (activated * up_pre).astype(BF16).astype(F32)
    share = score[...]
    gate_scale[...] = share * up_pre * gate_sig * (1.0 + gate_pre * (1.0 - gate_sig))
    up_scale[...] = share * activated
    logit_scale[...] = hidden * (share * (1.0 - share))
    scored[...] = (hidden * share).astype(BF16).T
    scales = gate_scale, up_scale, logit_scale
    section, sections = lax.axis_index("section"), lax.axis_size("section")

    @pl.when(section == sections - 1)
    def _():
        push_back(grad, back_proj[...], scales, gate_vector, pieces, columns, out)

    @pl.when(section < sections - 1)
    def _():
        out[...] = grad[...]


def tick_kernel(offsets, section, grad, held, down, gate_vector, a, b, c, *rest):
    pieces, out = pair_up(rest[:-1]), rest[-1]

    here = lax.axis_index("section") == section

    @pl.when(jnp.logical_not(here))
    def _():
        out[...] = held[...]

    @pl.when(here)
    def _():
        depth = pieces[0][0].shape[0]
        columns = [piece_columns(offset, "dp", depth) for offset in offsets]
        back_proj = dot(grad[...], down[...], TURNED)
        push_back(grad, back_proj, (a, b, c), gate_vector, pieces, columns, out)


def block_rows(bits, rest, units):
    return pl.ds(pl.multiple_of((rest * 4 + 2 * bits[1] + bits[0]) * units, units), units)


def own_bits():
    me = lax.axis_index("dp")
    return me % 2, me // 2 % 2


def split_kernel(scored, *out):
    size = lax.axis_size("dp")
    units = scored.shape[0] // size
    own = own_bits()
    for bit in range(2):
        for second in range(2):
            for rest in range(size // 4):
                bits = (1 - own[0], second) if bit == 0 else (second, 1 - own[1])
                start = (second * (size // 4) + rest) * units
                out[bit][start : start + units, :] = scored[block_rows(bits, rest, units), :]


def products_kernel(scored, grad, *rest):
    theirs, partners, sends, keeps = rest[:2], rest[2:4], rest[4:6], rest[6:]
    size = lax.axis_size("dp")
    units = scored.shape[0] // size
    half, width = sends[0].shape
    own = own_bits()
    for bit in range(2):
        columns = slice(bit * width, (bit + 1) * width)
        mine = grad[:, columns]

        def rows(second):
            bits = (own[0], second) if bit == 0 else (second, own[1])
            blocks = [scored[block_rows(bits, rest, units), :] for rest in range(size // 4)]
            where = pl.ds(pl.multiple_of(second * half, half), half)
            left = jnp.concatenate(blocks, axis=0)
            return dot(left, mine, PLAIN) + dot(theirs[bit][where, :], partners[bit][...], PLAIN)

        sends[bit][...] = rows(1 - own[1 - bit]).astype(BF16)
        keeps[bit][...] = rows(own[1 - bit])


def combine_kernel(bit, count, *refs):
    keeps, gots, (send, kept) = refs[:count], refs[count : 2 * count], refs[2 * count :]
    width = keeps[0].shape[1]
    half = send.shape[0]
    own = lax.axis_index("dp") >> bit & 1
    for i, (keep, got) in enumerate(zip(keeps, gots)):
        columns = slice(i * width, (i + 1) * width)

        def rows(which):
            where = pl.ds(pl.multiple_of(which * half, half), half)
            return keep[where, :] + got[where, :].astype(F32)

        send[:, columns] = rows(1 - own).astype(BF16)
        kept[:, columns] = rows(own).astype(kept.dtype)


def finish_kernel(factor, first, second, out):
    out[...] = (first[...].astype(F32) + second[...].astype(F32)) * factor


def along(bit, *values):
    pairs = [(i, i ^ 1 << bit) for i in range(lax.axis_size("dp"))]
    return [lax.ppermute(v, "dp", pairs) for v in values]


def call(kernel, name, outs, macs, *args):
    return pl.pallas_call(
        kernel,
        out_shape=outs,
        in_specs=[VMEM] * len(args),
        out_specs=[VMEM] * len(outs),
        compiler_params=params(),
        cost_estimate=cost(macs, *args),
        name=name,
    )(*args)


def swap_scored(scored):
    half = jax.ShapeDtypeStruct((scored.shape[0] // 2, scored.shape[1]), BF16)
    to_first, to_second = call(split_kernel, "split", [half] * 2, 0, scored)
    return [*along(0, to_first), *along(1, to_second)]


def reduce_rows(scored, theirs, grad):
    size = lax.axis_size("dp")
    rows, width = scored.shape[0] // 4, grad.shape[1]
    shape = jax.ShapeDtypeStruct
    partners = [*along(0, grad[:, : width // 2]), *along(1, grad[:, width // 2 :])]
    half = (rows, width // 2)
    outs = [shape(half, BF16)] * 2 + [shape(half, F32)] * 2
    macs = 4 * rows * scored.shape[1] * width
    *sends, keep_a, keep_b = call(
        products_kernel, "products", outs, macs, scored, grad, *theirs, *partners
    )
    keeps = [keep_a, keep_b]
    gots = [*along(1, sends[0]), *along(0, sends[1])]
    for bit in range(size.bit_length() - 2, 1, -1):
        rows //= 2
        outs = [shape((rows, width), BF16), shape((rows, width), BF16 if bit == 2 else F32)]
        kernel = functools.partial(combine_kernel, bit, len(keeps))
        send, keep = call(kernel, "combine", outs, 0, *keeps, *gots)
        if bit == 2:
            return send, keep
        keeps, gots = [keep], along(bit, send)


def to_layer(value, flip):
    sections, size = lax.axis_size("section"), lax.axis_size("dp")
    pairs = [
        (s * size + d, (s - 1) % sections * size + (d ^ flip))
        for s in range(sections)
        for d in range(size)
    ]
    return lax.ppermute(value, ("section", "dp"), pairs)


def on_device(stash, cotangent, gate_weight, up_weight, down_weight, shared_gate):
    sections = lax.axis_size("section")
    replicas = lax.axis_size("dp")
    local_rows, model_width = stash.shape[1:]
    depth = gate_weight.shape[1]
    down_full = down_weight[0]
    hidden_units = down_full.shape[0]

    shape = jax.ShapeDtypeStruct
    small = shape((local_rows, hidden_units), F32)
    cotangents = gather_to_ends(cotangent, "section")
    blocks, block_offsets = next(cotangents)
    own_rows = stash[0]

    def between(step, i, moving):
        nonlocal blocks, own_rows
        if step == 1 and i == 1:
            blocks, _ = next(cotangents, (blocks, None))
        if step == 2 and i == 0:
            own_rows, *moving = after((own_rows, *moving))
            mirrored = [(k, sections - 1 - k) for k in range(sections)]
            own_rows = lax.ppermute(own_rows, "section", mirrored)
        if step == 2 and i == 1:
            moving, blocks = after((moving, blocks))
            blocks, _ = next(cotangents, (list(blocks), None))
        if step == 3 and i == 1:
            moving, blocks = after((moving, blocks))
        if step == replicas // 2 and i == 0:
            moving, own_rows = after((moving, own_rows))
        return moving

    pieces, offsets = gather_ring([gate_weight[0], up_weight[0]], "dp", between)
    for blocks, _ in cotangents:
        pass
    seeded, back_proj = pl.pallas_call(
        functools.partial(prepare_kernel, block_offsets),
        out_shape=[shape((local_rows, model_width), BF16), small],
        in_specs=[VMEM] * (1 + len(blocks)),
        out_specs=[VMEM] * 2,
        compiler_params=params(),
        cost_estimate=cost(local_rows * model_width * hidden_units, down_full),
        name="prepare",
    )(down_full, *blocks)
    score = pl.pallas_call(
        score_kernel,
        out_shape=shape((local_rows, 1), F32),
        in_specs=[VMEM] * 2,
        out_specs=VMEM,
        compiler_params=params(),
        cost_estimate=cost(local_rows * model_width, own_rows),
        name="score",
    )(own_rows, shared_gate)

    if depth % 128:
        size = replicas
        place = ring_place(lax.axis_index("dp"), size)
        joined = [jnp.zeros((depth * replicas, hidden_units), BF16)] * 2
        for offset, piece in zip(offsets, pieces):
            start = ring_member((place + offset + size) % size, size) * depth
            joined = [lax.dynamic_update_slice(j, p, (start, 0)) for j, p in zip(joined, piece)]
        pieces, offsets = [joined], [None]
    flat = [v for piece in pieces for v in piece]

    outgoing, *scales, scored = pl.pallas_call(
        functools.partial(first_kernel, offsets),
        out_shape=[
            shape((local_rows, model_width), BF16),
            small,
            small,
            small,
            shape((hidden_units, local_rows), BF16),
        ],
        in_specs=[VMEM] * (5 + len(flat)),
        out_specs=[VMEM] * 5,
        compiler_params=params(),
        cost_estimate=cost(4 * local_rows * model_width * hidden_units, *flat),
        name="first_tick",
    )(own_rows, score, back_proj, seeded, shared_gate, *flat)
    around = [(i, (i + 1) % sections) for i in range(sections)]
    scored = lax.ppermute(scored, "section", around)

    def tick(section, grad, held):
        return pl.pallas_call(
            functools.partial(tick_kernel, offsets, section),
            out_shape=shape((local_rows, model_width), BF16),
            in_specs=[VMEM] * (7 + len(flat)),
            out_specs=VMEM,
            compiler_params=params(),
            cost_estimate=cost(3 * local_rows * model_width * hidden_units, *flat),
            name="tick",
        )(grad, held, down_full, shared_gate, *scales, *flat)

    swap = [(i, i ^ 1) for i in range(sections)]
    for section in range(sections - 2, -1, -1):
        if section == 0:
            reduced = reduce_rows(scored, theirs, outgoing)
        if section == sections - 3:
            outgoing, scored = after((outgoing, scored))
        pairs = swap if section == sections - 2 else [(section + 1, section)]
        grad = lax.ppermute(outgoing, "section", pairs)
        if section == max(sections - 3, 0):
            grad, theirs = after((grad, swap_scored(scored)))
        outgoing = tick(section, grad, outgoing)

    send, keep = reduced
    kernel = functools.partial(finish_kernel, (local_rows * replicas) ** (-0.5))
    outs = [shape(keep.shape, F32)]
    summed = call(kernel, "finish", outs, 0, to_layer(send, 4), to_layer(keep, 0))[0]
    return (outgoing[None], summed[None])


def solution(mesh):
    placed = (
        P("section", "dp", None),
        P("dp", "section"),
        P("section", "dp", None),
        P("section", "dp", None),
        P("section", None, None),
        P("section", None),
    )
    return jax.shard_map(
        on_device,
        mesh=mesh,
        in_specs=placed,
        out_specs=(P("section", "dp", None), P("section", "dp", None)),
        check_vma=False,
    )
```

```python
import functools

import jax
import jax.numpy as jnp
from jax import lax
from jax.experimental import pallas as pl
from jax.experimental.pallas import tpu as pltpu
from jax.sharding import PartitionSpec as P

F32, BF16 = jnp.float32, jnp.bfloat16
PLAIN = (((1,), (0,)), ((), ()))
TURNED = (((1,), (1,)), ((), ()))
VMEM = pl.BlockSpec(memory_space=pltpu.VMEM)
LIMIT = 16 * 2**20


def dot(left, right, dims):
    return lax.dot_general(left, right, dims, preferred_element_type=F32)


def params():
    return pltpu.CompilerParams(vmem_limit_bytes=LIMIT)


def cost(macs, *arrays):
    moved = sum(a.size * a.dtype.itemsize for a in arrays)
    return pl.CostEstimate(flops=2 * macs, bytes_accessed=moved, transcendentals=0)


def ring_place(index, size):
    return jnp.where(index % 2 == 0, index // 2, size - 1 - index // 2)


def ring_member(place, size):
    return jnp.where(place < (size + 1) // 2, 2 * place, 2 * (size - 1 - place) + 1)


def ring_pairs(size):
    order = list(range(0, size, 2)) + list(range(1, size, 2))[::-1]
    ahead = [(order[i], order[(i + 1) % size]) for i in range(size)]
    return ahead, [(b, a) for a, b in ahead]


def gather_ring(arrays, axis, between):
    size = lax.axis_size(axis)
    ahead, back = ring_pairs(size)
    pieces, offsets = [list(arrays)], [0]
    moving = [(v, v) for v in arrays]
    for step in range(1, (size - 1) // 2 + 1):
        moved = []
        for i, (v, w) in enumerate(moving):
            v, w = between(step, i, (v, w))
            both = lax.ppermute(v, axis, ahead), lax.ppermute(w, axis, back)
            moved.append(lax.optimization_barrier(both))
        moving = moved
        pieces += [[v for v, _ in moving], [w for _, w in moving]]
        offsets += [-step, step]
    if size % 2 == 0:
        (v, _), (_, w) = between(size // 2, 0, moving[0]), between(size // 2, 1, moving[1])
        pieces.append([lax.ppermute(v, axis, ahead), lax.ppermute(w, axis, back)])
        offsets.append(size // 2)
    return pieces, offsets


def gather_to_ends(x, axis):
    size = lax.axis_size(axis)
    steps = [1 << place for place in range(size.bit_length() - 1)][::-1]
    needed = [{0, size - 1}]
    for stride in steps[::-1]:
        needed.append(needed[-1] | {i ^ stride for i in needed[-1]})
    held, offsets = [x], [0]
    yield held, offsets
    for stride, wanted in zip(steps, needed[-2::-1]):
        pairs = [(i ^ stride, i) for i in sorted(wanted)]
        held += [lax.ppermute(block, axis, pairs) for block in list(held)]
        offsets += [offset ^ stride for offset in offsets]
        yield held, offsets


def after(values, *others):
    return lax.optimization_barrier((values, others))[0]


def piece_columns(offset, axis, depth):
    if offset is None:
        return slice(0, depth)
    size = lax.axis_size(axis)
    place = (ring_place(lax.axis_index(axis), size) + (offset + size)) % size
    return pl.ds(pl.multiple_of(ring_member(place, size) * depth, depth), depth)


def push_back(grad_ref, back_proj, scales, gate_vector, turned, pieces, columns, out_ref):
    gate_scale, up_scale, logit_scale = scales
    logit = jnp.sum(back_proj * logit_scale[...], axis=1, keepdims=True)
    gate_grad = (back_proj * gate_scale[...]).astype(BF16)
    up_grad = (back_proj * up_scale[...]).astype(BF16)
    for i, (where, (gate, up)) in enumerate(zip(columns, pieces)):
        dims = PLAIN if i < turned else TURNED
        through = dot(gate_grad, gate[...], dims) + dot(up_grad, up[...], dims)
        out_ref[:, where] = (
            grad_ref[:, where].astype(F32) + through + logit * gate_vector[:, where].astype(F32)
        ).astype(BF16)


def turn_kernel(*refs):
    half = len(refs) // 2
    for value, out in zip(refs[:half], refs[half:]):
        out[...] = value[...].T


def pair_up(refs):
    return [refs[i : i + 2] for i in range(0, len(refs), 2)]


def score_kernel(rows, gate_vector, score):
    logit = jnp.sum(
        rows[...].astype(F32) * gate_vector[...].astype(F32), axis=1, keepdims=True
    )
    score[...] = jax.nn.sigmoid(logit)


def prepare_kernel(offsets, down, *rest):
    blocks, (seeded, back_proj) = rest[:-2], rest[-2:]
    sections = lax.axis_size("section")
    is_last = lax.axis_index("section") == sections - 1
    width = blocks[0].shape[1]

    def lay(flip):
        for offset, block in zip(offsets, blocks):
            place = offset ^ flip
            seeded[:, place * width : (place + 1) * width] = block[...]

    pl.when(is_last)(lambda: lay(sections - 1))
    pl.when(jnp.logical_not(is_last))(lambda: lay(0))
    back_proj[...] = dot(seeded[...], down[...], TURNED)


def first_kernel(offsets, turned, rows, score, back_proj, grad, gate_vector, *rest):
    pieces, rest = pair_up(rest[: 2 * len(offsets)]), rest[2 * len(offsets) :]
    turned_pieces, rest = pair_up(rest[: 2 * turned]), rest[2 * turned :]
    out, gate_scale, up_scale, logit_scale, scored = rest
    depth = pieces[0][0].shape[0]
    columns = [piece_columns(offset, "dp", depth) for offset in offsets]
    gate_pre = up_pre = 0.0
    for where, (gate, up) in zip(columns, pieces):
        block = rows[:, where]
        gate_pre += dot(block, gate[...], PLAIN)
        up_pre += dot(block, up[...], PLAIN)
    gate_sig = jax.nn.sigmoid(gate_pre)
    activated = gate_pre * gate_sig
    hidden = (activated * up_pre).astype(BF16).astype(F32)
    share = score[...]
    gate_scale[...] = share * up_pre * gate_sig * (1.0 + gate_pre * (1.0 - gate_sig))
    up_scale[...] = share * activated
    logit_scale[...] = hidden * (share * (1.0 - share))
    scored[...] = (hidden * share).astype(BF16).T
    scales = gate_scale, up_scale, logit_scale
    section, sections = lax.axis_index("section"), lax.axis_size("section")

    @pl.when(section == sections - 1)
    def _():
        back = turned_pieces + pieces[turned:]
        push_back(grad, back_proj[...], scales, gate_vector, turned, back, columns, out)

    @pl.when(section < sections - 1)
    def _():
        out[...] = grad[...]


def tick_kernel(offsets, turned, section, grad, held, down, gate_vector, a, b, c, *rest):
    pieces, out = pair_up(rest[:-1]), rest[-1]

    here = lax.axis_index("section") == section

    @pl.when(jnp.logical_not(here))
    def _():
        out[...] = held[...]

    @pl.when(here)
    def _():
        depth = pieces[0][0].shape[1 if turned else 0]
        columns = [piece_columns(offset, "dp", depth) for offset in offsets]
        back_proj = dot(grad[...], down[...], PLAIN if turned else TURNED)
        push_back(grad, back_proj, (a, b, c), gate_vector, turned, pieces, columns, out)


def block_rows(bits, rest, units):
    return pl.ds(pl.multiple_of((rest * 4 + 2 * bits[1] + bits[0]) * units, units), units)


def own_bits():
    me = lax.axis_index("dp")
    return me % 2, me // 2 % 2


def split_kernel(scored, *out):
    size = lax.axis_size("dp")
    units = scored.shape[0] // size
    own = own_bits()
    for bit in range(2):
        for second in range(2):
            for rest in range(size // 4):
                bits = (1 - own[0], second) if bit == 0 else (second, 1 - own[1])
                start = (second * (size // 4) + rest) * units
                out[bit][start : start + units, :] = scored[block_rows(bits, rest, units), :]


def products_kernel(scored, grad, *rest):
    theirs, partners, sends, keeps = rest[:2], rest[2:4], rest[4:6], rest[6:]
    size = lax.axis_size("dp")
    units = scored.shape[0] // size
    half, width = sends[0].shape
    own = own_bits()
    for bit in range(2):
        columns = slice(bit * width, (bit + 1) * width)
        mine = grad[:, columns]

        def rows(second):
            bits = (own[0], second) if bit == 0 else (second, own[1])
            blocks = [scored[block_rows(bits, rest, units), :] for rest in range(size // 4)]
            where = pl.ds(pl.multiple_of(second * half, half), half)
            left = jnp.concatenate(blocks, axis=0)
            return dot(left, mine, PLAIN) + dot(theirs[bit][where, :], partners[bit][...], PLAIN)

        sends[bit][...] = rows(1 - own[1 - bit]).astype(BF16)
        keeps[bit][...] = rows(own[1 - bit])


def combine_kernel(bit, count, *refs):
    keeps, gots, (send, kept) = refs[:count], refs[count : 2 * count], refs[2 * count :]
    width = keeps[0].shape[1]
    half = send.shape[0]
    own = lax.axis_index("dp") >> bit & 1
    for i, (keep, got) in enumerate(zip(keeps, gots)):
        columns = slice(i * width, (i + 1) * width)

        def rows(which):
            where = pl.ds(pl.multiple_of(which * half, half), half)
            return keep[where, :] + got[where, :].astype(F32)

        send[:, columns] = rows(1 - own).astype(BF16)
        kept[:, columns] = rows(own).astype(kept.dtype)


def finish_kernel(factor, first, second, out):
    out[...] = (first[...].astype(F32) + second[...].astype(F32)) * factor


def along(bit, *values):
    pairs = [(i, i ^ 1 << bit) for i in range(lax.axis_size("dp"))]
    return [lax.ppermute(v, "dp", pairs) for v in values]


def call(kernel, name, outs, macs, *args):
    return pl.pallas_call(
        kernel,
        out_shape=outs,
        in_specs=[VMEM] * len(args),
        out_specs=[VMEM] * len(outs),
        compiler_params=params(),
        cost_estimate=cost(macs, *args),
        name=name,
    )(*args)


def swap_scored(scored):
    half = jax.ShapeDtypeStruct((scored.shape[0] // 2, scored.shape[1]), BF16)
    to_first, to_second = call(split_kernel, "split", [half] * 2, 0, scored)
    return [*along(0, to_first), *along(1, to_second)]


def reduce_rows(scored, theirs, grad):
    size = lax.axis_size("dp")
    rows, width = scored.shape[0] // 4, grad.shape[1]
    shape = jax.ShapeDtypeStruct
    partners = [*along(0, grad[:, : width // 2]), *along(1, grad[:, width // 2 :])]
    half = (rows, width // 2)
    outs = [shape(half, BF16)] * 2 + [shape(half, F32)] * 2
    macs = 4 * rows * scored.shape[1] * width
    *sends, keep_a, keep_b = call(
        products_kernel, "products", outs, macs, scored, grad, *theirs, *partners
    )
    keeps = [keep_a, keep_b]
    gots = [*along(1, sends[0]), *along(0, sends[1])]
    for bit in range(size.bit_length() - 2, 1, -1):
        rows //= 2
        outs = [shape((rows, width), BF16), shape((rows, width), BF16 if bit == 2 else F32)]
        kernel = functools.partial(combine_kernel, bit, len(keeps))
        send, keep = call(kernel, "combine", outs, 0, *keeps, *gots)
        if bit == 2:
            return send, keep
        keeps, gots = [keep], along(bit, send)


def to_layer(value, flip):
    sections, size = lax.axis_size("section"), lax.axis_size("dp")
    pairs = [
        (s * size + d, (s - 1) % sections * size + (d ^ flip))
        for s in range(sections)
        for d in range(size)
    ]
    return lax.ppermute(value, ("section", "dp"), pairs)


def on_device(stash, cotangent, gate_weight, up_weight, down_weight, shared_gate):
    sections = lax.axis_size("section")
    replicas = lax.axis_size("dp")
    local_rows, model_width = stash.shape[1:]
    depth = gate_weight.shape[1]
    down_full = down_weight[0]
    hidden_units = down_full.shape[0]

    shape = jax.ShapeDtypeStruct
    small = shape((local_rows, hidden_units), F32)
    cotangents = gather_to_ends(cotangent, "section")
    blocks, block_offsets = next(cotangents)
    own_rows = stash[0]

    def between(step, i, moving):
        nonlocal blocks, own_rows
        if step == 1 and i == 1:
            blocks, _ = next(cotangents, (blocks, None))
        if step == 2 and i == 0:
            own_rows, *moving = after((own_rows, *moving))
            mirrored = [(k, sections - 1 - k) for k in range(sections)]
            own_rows = lax.ppermute(own_rows, "section", mirrored)
        if step == 2 and i == 1:
            moving, blocks = after((moving, blocks))
            blocks, _ = next(cotangents, (list(blocks), None))
        if step == 3 and i == 1:
            moving, blocks = after((moving, blocks))
        if step == replicas // 2 and i == 0:
            moving, own_rows = after((moving, own_rows))
        return moving

    pieces, offsets = gather_ring([gate_weight[0], up_weight[0]], "dp", between)
    for blocks, _ in cotangents:
        pass
    turned = 0 if depth % 128 else len(pieces) - 1
    down_back = down_full
    if turned:
        outs = [shape(down_full.shape[::-1], BF16)]
        down_back = call(turn_kernel, "turn_down", outs, 0, down_full)[0]
    outs = [shape((hidden_units, depth), BF16)] * 2
    turned_pieces = [call(turn_kernel, "turn", outs, 0, *piece) for piece in pieces[:turned]]
    seeded, back_proj = pl.pallas_call(
        functools.partial(prepare_kernel, block_offsets),
        out_shape=[shape((local_rows, model_width), BF16), small],
        in_specs=[VMEM] * (1 + len(blocks)),
        out_specs=[VMEM] * 2,
        compiler_params=params(),
        cost_estimate=cost(local_rows * model_width * hidden_units, down_full),
        name="prepare",
    )(down_full, *blocks)
    score = pl.pallas_call(
        score_kernel,
        out_shape=shape((local_rows, 1), F32),
        in_specs=[VMEM] * 2,
        out_specs=VMEM,
        compiler_params=params(),
        cost_estimate=cost(local_rows * model_width, own_rows),
        name="score",
    )(own_rows, shared_gate)

    if depth % 128:
        size = replicas
        place = ring_place(lax.axis_index("dp"), size)
        joined = [jnp.zeros((depth * replicas, hidden_units), BF16)] * 2
        for offset, piece in zip(offsets, pieces):
            start = ring_member((place + offset + size) % size, size) * depth
            joined = [lax.dynamic_update_slice(j, p, (start, 0)) for j, p in zip(joined, piece)]
        pieces, offsets = [joined], [None]
    flat = [v for piece in pieces for v in piece]
    flat_turned = [v for piece in turned_pieces for v in piece]
    flat_back = flat_turned + flat[2 * turned :]

    outgoing, *scales, scored = pl.pallas_call(
        functools.partial(first_kernel, offsets, turned),
        out_shape=[
            shape((local_rows, model_width), BF16),
            small,
            small,
            small,
            shape((hidden_units, local_rows), BF16),
        ],
        in_specs=[VMEM] * (5 + len(flat) + 2 * turned),
        out_specs=[VMEM] * 5,
        compiler_params=params(),
        cost_estimate=cost(4 * local_rows * model_width * hidden_units, *flat),
        name="first_tick",
    )(own_rows, score, back_proj, seeded, shared_gate, *flat, *flat_turned)
    around = [(i, (i + 1) % sections) for i in range(sections)]
    scored = lax.ppermute(scored, "section", around)

    def tick(section, grad, held):
        return pl.pallas_call(
            functools.partial(tick_kernel, offsets, turned, section),
            out_shape=shape((local_rows, model_width), BF16),
            in_specs=[VMEM] * (7 + len(flat)),
            out_specs=VMEM,
            compiler_params=params(),
            cost_estimate=cost(3 * local_rows * model_width * hidden_units, *flat),
            name="tick",
        )(grad, held, down_back, shared_gate, *scales, *flat_back)

    swap = [(i, i ^ 1) for i in range(sections)]
    for section in range(sections - 2, -1, -1):
        if section == 0:
            reduced = reduce_rows(scored, theirs, outgoing)
        if section == sections - 3:
            outgoing, scored = after((outgoing, scored))
        pairs = swap if section == sections - 2 else [(section + 1, section)]
        grad = lax.ppermute(outgoing, "section", pairs)
        if section == max(sections - 3, 0):
            grad, theirs = after((grad, swap_scored(scored)))
        outgoing = tick(section, grad, outgoing)

    send, keep = reduced
    kernel = functools.partial(finish_kernel, (local_rows * replicas) ** (-0.5))
    outs = [shape(keep.shape, F32)]
    summed = call(kernel, "finish", outs, 0, to_layer(send, 4), to_layer(keep, 0))[0]
    return (outgoing[None], summed[None])


def solution(mesh):
    placed = (
        P("section", "dp", None),
        P("dp", "section"),
        P("section", "dp", None),
        P("section", "dp", None),
        P("section", None, None),
        P("section", None),
    )
    return jax.shard_map(
        on_device,
        mesh=mesh,
        in_specs=placed,
        out_specs=(P("section", "dp", None), P("section", "dp", None)),
        check_vma=False,
    )
```

```python
import functools

import jax
import jax.numpy as jnp
from jax import lax
from jax.experimental import pallas as pl
from jax.experimental.pallas import tpu as pltpu
from jax.sharding import PartitionSpec as P

F32, BF16 = jnp.float32, jnp.bfloat16
PLAIN = (((1,), (0,)), ((), ()))
TURNED = (((1,), (1,)), ((), ()))
VMEM = pl.BlockSpec(memory_space=pltpu.VMEM)
LIMIT = 16 * 2**20


def dot(left, right, dims):
    return lax.dot_general(left, right, dims, preferred_element_type=F32)


def params():
    return pltpu.CompilerParams(vmem_limit_bytes=LIMIT)


def cost(macs, *arrays):
    moved = sum(a.size * a.dtype.itemsize for a in arrays)
    return pl.CostEstimate(flops=2 * macs, bytes_accessed=moved, transcendentals=0)


def ring_place(index, size):
    return jnp.where(index % 2 == 0, index // 2, size - 1 - index // 2)


def ring_member(place, size):
    return jnp.where(place < (size + 1) // 2, 2 * place, 2 * (size - 1 - place) + 1)


def ring_pairs(size):
    order = list(range(0, size, 2)) + list(range(1, size, 2))[::-1]
    ahead = [(order[i], order[(i + 1) % size]) for i in range(size)]
    return ahead, [(b, a) for a, b in ahead]


def gather_ring(arrays, axis, between):
    size = lax.axis_size(axis)
    ahead, back = ring_pairs(size)
    pieces, offsets = [list(arrays)], [0]
    moving = [(v, v) for v in arrays]
    for step in range(1, (size - 1) // 2 + 1):
        moved = []
        for i, (v, w) in enumerate(moving):
            v, w = between(step, i, (v, w))
            both = lax.ppermute(v, axis, ahead), lax.ppermute(w, axis, back)
            moved.append(lax.optimization_barrier(both))
        moving = moved
        pieces += [[v for v, _ in moving], [w for _, w in moving]]
        offsets += [-step, step]
    if size % 2 == 0:
        (v, _), (_, w) = between(size // 2, 0, moving[0]), between(size // 2, 1, moving[1])
        pieces.append([lax.ppermute(v, axis, ahead), lax.ppermute(w, axis, back)])
        offsets.append(size // 2)
    return pieces, offsets


def gather_blocks(x, axis):
    size = lax.axis_size(axis)
    held, offsets = [x], [0]
    yield held, offsets
    for place in range(size.bit_length() - 1)[::-1]:
        stride = 1 << place
        pairs = [(i, i ^ stride) for i in range(size)]
        held += [lax.ppermute(block, axis, pairs) for block in list(held)]
        offsets += [offset ^ stride for offset in offsets]
        yield held, offsets


def after(values, *others):
    return lax.optimization_barrier((values, others))[0]


def piece_columns(offset, axis, depth):
    if offset is None:
        return slice(0, depth)
    size = lax.axis_size(axis)
    place = (ring_place(lax.axis_index(axis), size) + (offset + size)) % size
    return pl.ds(pl.multiple_of(ring_member(place, size) * depth, depth), depth)


def push_back(grad_ref, back_proj, scales, gate_vector, turned, pieces, columns, out_ref):
    gate_scale, up_scale, logit_scale = scales
    logit = jnp.sum(back_proj * logit_scale[...], axis=1, keepdims=True)
    gate_grad = (back_proj * gate_scale[...]).astype(BF16)
    up_grad = (back_proj * up_scale[...]).astype(BF16)
    for i, (where, (gate, up)) in enumerate(zip(columns, pieces)):
        dims = PLAIN if i < turned else TURNED
        through = dot(gate_grad, gate[...], dims) + dot(up_grad, up[...], dims)
        out_ref[:, where] = (
            grad_ref[:, where].astype(F32) + through + logit * gate_vector[:, where].astype(F32)
        ).astype(BF16)


def turn_kernel(*refs):
    half = len(refs) // 2
    for value, out in zip(refs[:half], refs[half:]):
        out[...] = value[...].T


def pair_up(refs):
    return [refs[i : i + 2] for i in range(0, len(refs), 2)]


def score_kernel(rows, gate_vector, score):
    logit = jnp.sum(
        rows[...].astype(F32) * gate_vector[...].astype(F32), axis=1, keepdims=True
    )
    score[...] = jax.nn.sigmoid(logit)


def prepare_kernel(offsets, down, *rest):
    blocks, (seeded, back_proj) = rest[:-2], rest[-2:]
    sections = lax.axis_size("section")
    is_last = lax.axis_index("section") == sections - 1
    width = blocks[0].shape[1]

    def lay(flip):
        for offset, block in zip(offsets, blocks):
            place = offset ^ flip
            seeded[:, place * width : (place + 1) * width] = block[...]

    pl.when(is_last)(lambda: lay(sections - 1))
    pl.when(jnp.logical_not(is_last))(lambda: lay(0))
    back_proj[...] = dot(seeded[...], down[...], TURNED)


def first_kernel(offsets, turned, rows, score, back_proj, grad, gate_vector, *rest):
    pieces, rest = pair_up(rest[: 2 * len(offsets)]), rest[2 * len(offsets) :]
    turned_pieces, rest = pair_up(rest[: 2 * turned]), rest[2 * turned :]
    out, gate_scale, up_scale, logit_scale, scored = rest
    depth = pieces[0][0].shape[0]
    columns = [piece_columns(offset, "dp", depth) for offset in offsets]
    gate_pre = up_pre = 0.0
    for where, (gate, up) in zip(columns, pieces):
        block = rows[:, where]
        gate_pre += dot(block, gate[...], PLAIN)
        up_pre += dot(block, up[...], PLAIN)
    gate_sig = jax.nn.sigmoid(gate_pre)
    activated = gate_pre * gate_sig
    hidden = (activated * up_pre).astype(BF16).astype(F32)
    share = score[...]
    gate_scale[...] = share * up_pre * gate_sig * (1.0 + gate_pre * (1.0 - gate_sig))
    up_scale[...] = share * activated
    logit_scale[...] = hidden * (share * (1.0 - share))
    scored[...] = (hidden * share).astype(BF16).T
    scales = gate_scale, up_scale, logit_scale
    section, sections = lax.axis_index("section"), lax.axis_size("section")

    @pl.when(section == sections - 1)
    def _():
        back = turned_pieces + pieces[turned:]
        push_back(grad, back_proj[...], scales, gate_vector, turned, back, columns, out)

    @pl.when(section < sections - 1)
    def _():
        out[...] = grad[...]


def tick_kernel(offsets, turned, section, grad, held, down, gate_vector, a, b, c, *rest):
    pieces, out = pair_up(rest[:-1]), rest[-1]

    here = lax.axis_index("section") == section

    @pl.when(jnp.logical_not(here))
    def _():
        out[...] = held[...]

    @pl.when(here)
    def _():
        depth = pieces[0][0].shape[1 if turned else 0]
        columns = [piece_columns(offset, "dp", depth) for offset in offsets]
        back_proj = dot(grad[...], down[...], PLAIN if turned else TURNED)
        push_back(grad, back_proj, (a, b, c), gate_vector, turned, pieces, columns, out)


def block_rows(bits, rest, units):
    return pl.ds(pl.multiple_of((rest * 4 + 2 * bits[1] + bits[0]) * units, units), units)


def own_bits():
    me = lax.axis_index("dp")
    return me % 2, me // 2 % 2


def split_kernel(scored, *out):
    size = lax.axis_size("dp")
    units = scored.shape[0] // size
    own = own_bits()
    for bit in range(2):
        for second in range(2):
            for rest in range(size // 4):
                bits = (1 - own[0], second) if bit == 0 else (second, 1 - own[1])
                start = (second * (size // 4) + rest) * units
                out[bit][start : start + units, :] = scored[block_rows(bits, rest, units), :]


def products_kernel(scored, grad, *rest):
    theirs, partners, sends, keeps = rest[:2], rest[2:4], rest[4:6], rest[6:]
    size = lax.axis_size("dp")
    units = scored.shape[0] // size
    half, width = sends[0].shape
    own = own_bits()
    for bit in range(2):
        columns = slice(bit * width, (bit + 1) * width)
        mine = grad[:, columns]

        def rows(second):
            bits = (own[0], second) if bit == 0 else (second, own[1])
            blocks = [scored[block_rows(bits, rest, units), :] for rest in range(size // 4)]
            where = pl.ds(pl.multiple_of(second * half, half), half)
            left = jnp.concatenate(blocks, axis=0)
            return dot(left, mine, PLAIN) + dot(theirs[bit][where, :], partners[bit][...], PLAIN)

        sends[bit][...] = rows(1 - own[1 - bit]).astype(BF16)
        keeps[bit][...] = rows(own[1 - bit])


def combine_kernel(bit, count, *refs):
    keeps, gots, (send, kept) = refs[:count], refs[count : 2 * count], refs[2 * count :]
    width = keeps[0].shape[1]
    half = send.shape[0]
    own = lax.axis_index("dp") >> bit & 1
    for i, (keep, got) in enumerate(zip(keeps, gots)):
        columns = slice(i * width, (i + 1) * width)

        def rows(which):
            where = pl.ds(pl.multiple_of(which * half, half), half)
            return keep[where, :] + got[where, :].astype(F32)

        send[:, columns] = rows(1 - own).astype(BF16)
        kept[:, columns] = rows(own).astype(kept.dtype)


def finish_kernel(factor, first, second, out):
    out[...] = (first[...].astype(F32) + second[...].astype(F32)) * factor


def along(bit, *values):
    pairs = [(i, i ^ 1 << bit) for i in range(lax.axis_size("dp"))]
    return [lax.ppermute(v, "dp", pairs) for v in values]


def call(kernel, name, outs, macs, *args):
    return pl.pallas_call(
        kernel,
        out_shape=outs,
        in_specs=[VMEM] * len(args),
        out_specs=[VMEM] * len(outs),
        compiler_params=params(),
        cost_estimate=cost(macs, *args),
        name=name,
    )(*args)


def swap_scored(scored):
    half = jax.ShapeDtypeStruct((scored.shape[0] // 2, scored.shape[1]), BF16)
    to_first, to_second = call(split_kernel, "split", [half] * 2, 0, scored)
    return [*along(0, to_first), *along(1, to_second)]


def reduce_rows(scored, theirs, grad):
    size = lax.axis_size("dp")
    rows, width = scored.shape[0] // 4, grad.shape[1]
    shape = jax.ShapeDtypeStruct
    partners = [*along(0, grad[:, : width // 2]), *along(1, grad[:, width // 2 :])]
    half = (rows, width // 2)
    outs = [shape(half, BF16)] * 2 + [shape(half, F32)] * 2
    macs = 4 * rows * scored.shape[1] * width
    *sends, keep_a, keep_b = call(
        products_kernel, "products", outs, macs, scored, grad, *theirs, *partners
    )
    keeps = [keep_a, keep_b]
    gots = [*along(1, sends[0]), *along(0, sends[1])]
    for bit in range(size.bit_length() - 2, 1, -1):
        rows //= 2
        outs = [shape((rows, width), BF16), shape((rows, width), BF16 if bit == 2 else F32)]
        kernel = functools.partial(combine_kernel, bit, len(keeps))
        send, keep = call(kernel, "combine", outs, 0, *keeps, *gots)
        if bit == 2:
            return send, keep
        keeps, gots = [keep], along(bit, send)


def to_layer(value, flip):
    sections, size = lax.axis_size("section"), lax.axis_size("dp")
    pairs = [
        (s * size + d, (s - 1) % sections * size + (d ^ flip))
        for s in range(sections)
        for d in range(size)
    ]
    return lax.ppermute(value, ("section", "dp"), pairs)


def on_device(stash, cotangent, gate_weight, up_weight, down_weight, shared_gate):
    sections = lax.axis_size("section")
    replicas = lax.axis_size("dp")
    local_rows, model_width = stash.shape[1:]
    depth = gate_weight.shape[1]
    down_full = down_weight[0]
    hidden_units = down_full.shape[0]

    shape = jax.ShapeDtypeStruct
    small = shape((local_rows, hidden_units), F32)
    cotangents = gather_blocks(cotangent, "section")
    blocks, block_offsets = next(cotangents)
    own_rows = stash[0]

    last_step = replicas // 2

    def between(step, i, moving):
        nonlocal blocks, own_rows
        if step == 1 and i == 0:
            mirrored = [(k, sections - 1 - k) for k in range(sections)]
            own_rows = lax.ppermute(own_rows, "section", mirrored)
        if step == 1 and i == 1:
            blocks, _ = next(cotangents, (blocks, None))
        if step == 2 and i == 0:
            moving, blocks = after((moving, blocks))
        if step == last_step - 1 and i == 0:
            blocks, _ = next(cotangents, (list(blocks), None))
        if step == last_step - 1 and i == 1:
            moving, own_rows = after((moving, own_rows))
        if step == last_step and i == 0:
            moving, blocks = after((moving, blocks))
        return moving

    pieces, offsets = gather_ring([gate_weight[0], up_weight[0]], "dp", between)
    for blocks, _ in cotangents:
        pass
    turned = 0 if depth % 128 else len(pieces) - 1
    down_back = down_full
    if turned:
        outs = [shape(down_full.shape[::-1], BF16)]
        down_back = call(turn_kernel, "turn_down", outs, 0, down_full)[0]
    outs = [shape((hidden_units, depth), BF16)] * 2
    turned_pieces = [call(turn_kernel, "turn", outs, 0, *piece) for piece in pieces[:turned]]
    seeded, back_proj = pl.pallas_call(
        functools.partial(prepare_kernel, block_offsets),
        out_shape=[shape((local_rows, model_width), BF16), small],
        in_specs=[VMEM] * (1 + len(blocks)),
        out_specs=[VMEM] * 2,
        compiler_params=params(),
        cost_estimate=cost(local_rows * model_width * hidden_units, down_full),
        name="prepare",
    )(down_full, *blocks)
    score = pl.pallas_call(
        score_kernel,
        out_shape=shape((local_rows, 1), F32),
        in_specs=[VMEM] * 2,
        out_specs=VMEM,
        compiler_params=params(),
        cost_estimate=cost(local_rows * model_width, own_rows),
        name="score",
    )(own_rows, shared_gate)

    if depth % 128:
        size = replicas
        place = ring_place(lax.axis_index("dp"), size)
        joined = [jnp.zeros((depth * replicas, hidden_units), BF16)] * 2
        for offset, piece in zip(offsets, pieces):
            start = ring_member((place + offset + size) % size, size) * depth
            joined = [lax.dynamic_update_slice(j, p, (start, 0)) for j, p in zip(joined, piece)]
        pieces, offsets = [joined], [None]
    flat = [v for piece in pieces for v in piece]
    flat_turned = [v for piece in turned_pieces for v in piece]
    flat_back = flat_turned + flat[2 * turned :]

    outgoing, *scales, scored = pl.pallas_call(
        functools.partial(first_kernel, offsets, turned),
        out_shape=[
            shape((local_rows, model_width), BF16),
            small,
            small,
            small,
            shape((hidden_units, local_rows), BF16),
        ],
        in_specs=[VMEM] * (5 + len(flat) + 2 * turned),
        out_specs=[VMEM] * 5,
        compiler_params=params(),
        cost_estimate=cost(4 * local_rows * model_width * hidden_units, *flat),
        name="first_tick",
    )(own_rows, score, back_proj, seeded, shared_gate, *flat, *flat_turned)
    around = [(i, (i + 1) % sections) for i in range(sections)]
    scored = lax.ppermute(scored, "section", around)

    def tick(section, grad, held):
        return pl.pallas_call(
            functools.partial(tick_kernel, offsets, turned, section),
            out_shape=shape((local_rows, model_width), BF16),
            in_specs=[VMEM] * (7 + len(flat)),
            out_specs=VMEM,
            compiler_params=params(),
            cost_estimate=cost(3 * local_rows * model_width * hidden_units, *flat),
            name="tick",
        )(grad, held, down_back, shared_gate, *scales, *flat_back)

    swap = [(i, i ^ 1) for i in range(sections)]
    for section in range(sections - 2, -1, -1):
        if section == 0:
            reduced = reduce_rows(scored, theirs, outgoing)
        if section == sections - 3:
            outgoing, scored = after((outgoing, scored))
        pairs = swap if section % 2 == 0 else [(section + 1, section)]
        grad = lax.ppermute(outgoing, "section", pairs)
        if section == max(sections - 3, 0):
            theirs = swap_scored(scored)
        outgoing = tick(section, grad, outgoing)

    send, keep = reduced
    kernel = functools.partial(finish_kernel, (local_rows * replicas) ** (-0.5))
    outs = [shape(keep.shape, F32)]
    summed = call(kernel, "finish", outs, 0, to_layer(send, 4), to_layer(keep, 0))[0]
    return (outgoing[None], summed[None])


def solution(mesh):
    placed = (
        P("section", "dp", None),
        P("dp", "section"),
        P("section", "dp", None),
        P("section", "dp", None),
        P("section", None, None),
        P("section", None),
    )
    return jax.shard_map(
        on_device,
        mesh=mesh,
        in_specs=placed,
        out_specs=(P("section", "dp", None), P("section", "dp", None)),
        check_vma=False,
    )
```

```python
import functools

import jax
import jax.numpy as jnp
from jax import lax
from jax.experimental import pallas as pl
from jax.experimental.pallas import tpu as pltpu
from jax.sharding import PartitionSpec as P

F32, BF16 = jnp.float32, jnp.bfloat16
PLAIN = (((1,), (0,)), ((), ()))
TURNED = (((1,), (1,)), ((), ()))
VMEM = pl.BlockSpec(memory_space=pltpu.VMEM)
LIMIT = 16 * 2**20


def dot(left, right, dims):
    return lax.dot_general(left, right, dims, preferred_element_type=F32)


def params():
    return pltpu.CompilerParams(vmem_limit_bytes=LIMIT)


def cost(macs, *arrays):
    moved = sum(a.size * a.dtype.itemsize for a in arrays)
    return pl.CostEstimate(flops=2 * macs, bytes_accessed=moved, transcendentals=0)


def ring_place(index, size):
    return jnp.where(index % 2 == 0, index // 2, size - 1 - index // 2)


def ring_member(place, size):
    return jnp.where(place < (size + 1) // 2, 2 * place, 2 * (size - 1 - place) + 1)


def ring_pairs(size):
    order = list(range(0, size, 2)) + list(range(1, size, 2))[::-1]
    ahead = [(order[i], order[(i + 1) % size]) for i in range(size)]
    return ahead, [(b, a) for a, b in ahead]


def gather_ring(arrays, axis, between):
    size = lax.axis_size(axis)
    ahead, back = ring_pairs(size)
    pieces, offsets = [list(arrays)], [0]
    moving = [(v, v) for v in arrays]
    for step in range(1, (size - 1) // 2 + 1):
        moved = []
        for i, (v, w) in enumerate(moving):
            v, w = between(step, i, (v, w))
            both = lax.ppermute(v, axis, ahead), lax.ppermute(w, axis, back)
            moved.append(lax.optimization_barrier(both))
        moving = moved
        pieces += [[v for v, _ in moving], [w for _, w in moving]]
        offsets += [-step, step]
    if size % 2 == 0:
        (v, _), (_, w) = between(size // 2, 0, moving[0]), between(size // 2, 1, moving[1])
        pieces.append([lax.ppermute(v, axis, ahead), lax.ppermute(w, axis, back)])
        offsets.append(size // 2)
    return pieces, offsets


def gather_blocks(x, axis):
    size = lax.axis_size(axis)
    held, offsets = [x], [0]
    yield held, offsets
    for place in range(size.bit_length() - 1)[::-1]:
        stride = 1 << place
        pairs = [(i, i ^ stride) for i in range(size)]
        held += [lax.ppermute(block, axis, pairs) for block in list(held)]
        offsets += [offset ^ stride for offset in offsets]
        yield held, offsets


def after(values, *others):
    return lax.optimization_barrier((values, others))[0]


def piece_columns(offset, axis, depth):
    if offset is None:
        return slice(0, depth)
    size = lax.axis_size(axis)
    place = (ring_place(lax.axis_index(axis), size) + (offset + size)) % size
    return pl.ds(pl.multiple_of(ring_member(place, size) * depth, depth), depth)


def push_back(grad_ref, back_proj, scales, gate_vector, turned, pieces, columns, out_ref):
    gate_scale, up_scale, logit_scale = scales
    logit = jnp.sum(back_proj * logit_scale[...], axis=1, keepdims=True)
    gate_grad = (back_proj * gate_scale[...]).astype(BF16)
    up_grad = (back_proj * up_scale[...]).astype(BF16)
    for i, (where, (gate, up)) in enumerate(zip(columns, pieces)):
        dims = PLAIN if i < turned else TURNED
        through = dot(gate_grad, gate[...], dims) + dot(up_grad, up[...], dims)
        out_ref[:, where] = (
            grad_ref[:, where].astype(F32) + through + logit * gate_vector[:, where].astype(F32)
        ).astype(BF16)


def turn_kernel(*refs):
    half = len(refs) // 2
    for value, out in zip(refs[:half], refs[half:]):
        out[...] = value[...].T


def pair_up(refs):
    return [refs[i : i + 2] for i in range(0, len(refs), 2)]


def score_kernel(rows, gate_vector, score):
    logit = jnp.sum(
        rows[...].astype(F32) * gate_vector[...].astype(F32), axis=1, keepdims=True
    )
    score[...] = jax.nn.sigmoid(logit)


def prepare_kernel(offsets, down, *rest):
    blocks, (seeded, back_proj) = rest[:-2], rest[-2:]
    sections = lax.axis_size("section")
    is_last = lax.axis_index("section") == sections - 1
    width = blocks[0].shape[1]

    def lay(flip):
        for offset, block in zip(offsets, blocks):
            place = offset ^ flip
            seeded[:, place * width : (place + 1) * width] = block[...]

    pl.when(is_last)(lambda: lay(sections - 1))
    pl.when(jnp.logical_not(is_last))(lambda: lay(0))
    back_proj[...] = dot(seeded[...], down[...], TURNED)


def first_kernel(offsets, turned, rows, score, back_proj, grad, gate_vector, *rest):
    pieces, rest = pair_up(rest[: 2 * len(offsets)]), rest[2 * len(offsets) :]
    turned_pieces, rest = pair_up(rest[: 2 * turned]), rest[2 * turned :]
    out, gate_scale, up_scale, logit_scale, scored = rest
    depth = pieces[0][0].shape[0]
    columns = [piece_columns(offset, "dp", depth) for offset in offsets]
    gate_pre = up_pre = 0.0
    for where, (gate, up) in zip(columns, pieces):
        block = rows[:, where]
        gate_pre += dot(block, gate[...], PLAIN)
        up_pre += dot(block, up[...], PLAIN)
    gate_sig = jax.nn.sigmoid(gate_pre)
    activated = gate_pre * gate_sig
    hidden = (activated * up_pre).astype(BF16).astype(F32)
    share = score[...]
    gate_scale[...] = share * up_pre * gate_sig * (1.0 + gate_pre * (1.0 - gate_sig))
    up_scale[...] = share * activated
    logit_scale[...] = hidden * (share * (1.0 - share))
    scored[...] = (hidden * share).astype(BF16).T
    scales = gate_scale, up_scale, logit_scale
    section, sections = lax.axis_index("section"), lax.axis_size("section")

    @pl.when(section == sections - 1)
    def _():
        back = turned_pieces + pieces[turned:]
        push_back(grad, back_proj[...], scales, gate_vector, turned, back, columns, out)

    @pl.when(section < sections - 1)
    def _():
        out[...] = grad[...]


def tick_kernel(offsets, turned, section, grad, held, down, gate_vector, a, b, c, *rest):
    pieces, out = pair_up(rest[:-1]), rest[-1]

    here = lax.axis_index("section") == section

    @pl.when(jnp.logical_not(here))
    def _():
        out[...] = held[...]

    @pl.when(here)
    def _():
        depth = pieces[0][0].shape[1 if turned else 0]
        columns = [piece_columns(offset, "dp", depth) for offset in offsets]
        back_proj = dot(grad[...], down[...], PLAIN if turned else TURNED)
        push_back(grad, back_proj, (a, b, c), gate_vector, turned, pieces, columns, out)


def orders(size):
    top = size.bit_length() - 2
    return [0, 1, *range(top, 1, -1)], [top, 0, *range(top - 1, 0, -1)]


def own_bit(bit):
    return lax.axis_index("dp") >> bit & 1


def block_rows(order, first, second, rest, units):
    place = (first << order[0]) + (second << order[1])
    for i, bit in enumerate(order[2:]):
        place += (rest >> len(order) - 3 - i & 1) << bit
    return pl.ds(pl.multiple_of(place * units, units), units)


def split_kernel(scored, *out):
    size = lax.axis_size("dp")
    units = scored.shape[0] // size
    for order, half in zip(orders(size), out):
        for second in range(2):
            for rest in range(size // 4):
                start = (second * (size // 4) + rest) * units
                rows = block_rows(order, 1 - own_bit(order[0]), second, rest, units)
                half[start : start + units, :] = scored[rows, :]


def products_kernel(scored, grad, *rest):
    theirs, partners, sends, keeps = rest[:2], rest[2:4], rest[4:6], rest[6:]
    size = lax.axis_size("dp")
    units = scored.shape[0] // size
    half, width = sends[0].shape
    for i, order in enumerate(orders(size)):
        mine = grad[:, i * width : (i + 1) * width]

        def rows(second):
            own = own_bit(order[0])
            blocks = [
                scored[block_rows(order, own, second, rest, units), :] for rest in range(size // 4)
            ]
            where = pl.ds(pl.multiple_of(second * half, half), half)
            left = jnp.concatenate(blocks, axis=0)
            return dot(left, mine, PLAIN) + dot(theirs[i][where, :], partners[i][...], PLAIN)

        sends[i][...] = rows(1 - own_bit(order[1])).astype(BF16)
        keeps[i][...] = rows(own_bit(order[1]))


def combine_kernel(stage, *refs):
    keeps, gots, sends, kept = refs[:2], refs[2:4], refs[4:6], refs[6:]
    half, width = sends[0].shape
    for i, order in enumerate(orders(lax.axis_size("dp"))):
        own = own_bit(order[stage])

        def rows(which):
            where = pl.ds(pl.multiple_of(which * half, half), half)
            return keeps[i][where, :] + gots[i][where, :].astype(F32)

        sends[i][...] = rows(1 - own).astype(BF16)
        if len(kept) == 2:
            kept[i][...] = rows(own)
        else:
            kept[0][:, i * width : (i + 1) * width] = rows(own).astype(BF16)


def finish_kernel(factor, first, second, keep, out):
    width = first.shape[1]
    for i, got in enumerate((first, second)):
        columns = slice(i * width, (i + 1) * width)
        out[:, columns] = (got[...].astype(F32) + keep[:, columns].astype(F32)) * factor


def along(stage, values):
    size = lax.axis_size("dp")
    found = []
    for order, value in zip(orders(size), values):
        pairs = [(i, i ^ 1 << order[stage]) for i in range(size)]
        found.append(lax.ppermute(value, "dp", pairs))
    return found


def call(kernel, name, outs, macs, *args):
    return pl.pallas_call(
        kernel,
        out_shape=outs,
        in_specs=[VMEM] * len(args),
        out_specs=[VMEM] * len(outs),
        compiler_params=params(),
        cost_estimate=cost(macs, *args),
        name=name,
    )(*args)


def swap_scored(scored):
    half = jax.ShapeDtypeStruct((scored.shape[0] // 2, scored.shape[1]), BF16)
    return along(0, call(split_kernel, "split", [half] * 2, 0, scored))


def reduce_rows(scored, theirs, grad):
    stages = lax.axis_size("dp").bit_length() - 1
    rows, width = scored.shape[0] // 4, grad.shape[1]
    shape = jax.ShapeDtypeStruct
    partners = along(0, (grad[:, : width // 2], grad[:, width // 2 :]))
    half = (rows, width // 2)
    outs = [shape(half, BF16)] * 2 + [shape(half, F32)] * 2
    macs = 4 * rows * scored.shape[1] * width
    found = call(products_kernel, "products", outs, macs, scored, grad, *theirs, *partners)
    for stage in range(2, stages):
        gots = along(stage - 1, found[:2])
        rows //= 2
        half = (rows, width // 2)
        outs = [shape(half, BF16)] * 2 + [shape(half, F32)] * 2
        if stage == stages - 1:
            outs[2:] = [shape((rows, width), BF16)]
        kernel = functools.partial(combine_kernel, stage)
        found = call(kernel, "combine", outs, 0, *found[2:], *gots)
    return found


def to_layer(value, flip):
    sections, size = lax.axis_size("section"), lax.axis_size("dp")
    pairs = [
        (s * size + d, (s - 1) % sections * size + (d ^ flip))
        for s in range(sections)
        for d in range(size)
    ]
    return lax.ppermute(value, ("section", "dp"), pairs)


def on_device(stash, cotangent, gate_weight, up_weight, down_weight, shared_gate):
    sections = lax.axis_size("section")
    replicas = lax.axis_size("dp")
    local_rows, model_width = stash.shape[1:]
    depth = gate_weight.shape[1]
    down_full = down_weight[0]
    hidden_units = down_full.shape[0]

    shape = jax.ShapeDtypeStruct
    small = shape((local_rows, hidden_units), F32)
    cotangents = gather_blocks(cotangent, "section")
    blocks, block_offsets = next(cotangents)
    own_rows = stash[0]

    last_step = replicas // 2

    def between(step, i, moving):
        nonlocal blocks, own_rows
        if step == 1 and i == 0:
            mirrored = [(k, sections - 1 - k) for k in range(sections)]
            own_rows = lax.ppermute(own_rows, "section", mirrored)
        if step == 1 and i == 1:
            blocks, _ = next(cotangents, (blocks, None))
        if step == 2 and i == 0:
            moving, blocks = after((moving, blocks))
        if step == last_step - 1 and i == 0:
            blocks, _ = next(cotangents, (list(blocks), None))
        if step == last_step - 1 and i == 1:
            moving, own_rows = after((moving, own_rows))
        if step == last_step and i == 0:
            moving, blocks = after((moving, blocks))
        return moving

    pieces, offsets = gather_ring([gate_weight[0], up_weight[0]], "dp", between)
    for blocks, _ in cotangents:
        pass
    turned = 0 if depth % 128 else len(pieces) - 1
    down_back = down_full
    if turned:
        outs = [shape(down_full.shape[::-1], BF16)]
        down_back = call(turn_kernel, "turn_down", outs, 0, down_full)[0]
    outs = [shape((hidden_units, depth), BF16)] * 2
    turned_pieces = [call(turn_kernel, "turn", outs, 0, *piece) for piece in pieces[:turned]]
    seeded, back_proj = pl.pallas_call(
        functools.partial(prepare_kernel, block_offsets),
        out_shape=[shape((local_rows, model_width), BF16), small],
        in_specs=[VMEM] * (1 + len(blocks)),
        out_specs=[VMEM] * 2,
        compiler_params=params(),
        cost_estimate=cost(local_rows * model_width * hidden_units, down_full),
        name="prepare",
    )(down_full, *blocks)
    score = pl.pallas_call(
        score_kernel,
        out_shape=shape((local_rows, 1), F32),
        in_specs=[VMEM] * 2,
        out_specs=VMEM,
        compiler_params=params(),
        cost_estimate=cost(local_rows * model_width, own_rows),
        name="score",
    )(own_rows, shared_gate)

    if depth % 128:
        size = replicas
        place = ring_place(lax.axis_index("dp"), size)
        joined = [jnp.zeros((depth * replicas, hidden_units), BF16)] * 2
        for offset, piece in zip(offsets, pieces):
            start = ring_member((place + offset + size) % size, size) * depth
            joined = [lax.dynamic_update_slice(j, p, (start, 0)) for j, p in zip(joined, piece)]
        pieces, offsets = [joined], [None]
    flat = [v for piece in pieces for v in piece]
    flat_turned = [v for piece in turned_pieces for v in piece]
    flat_back = flat_turned + flat[2 * turned :]

    outgoing, *scales, scored = pl.pallas_call(
        functools.partial(first_kernel, offsets, turned),
        out_shape=[
            shape((local_rows, model_width), BF16),
            small,
            small,
            small,
            shape((hidden_units, local_rows), BF16),
        ],
        in_specs=[VMEM] * (5 + len(flat) + 2 * turned),
        out_specs=[VMEM] * 5,
        compiler_params=params(),
        cost_estimate=cost(4 * local_rows * model_width * hidden_units, *flat),
        name="first_tick",
    )(own_rows, score, back_proj, seeded, shared_gate, *flat, *flat_turned)
    around = [(i, (i + 1) % sections) for i in range(sections)]
    scored = lax.ppermute(scored, "section", around)

    def tick(section, grad, held):
        return pl.pallas_call(
            functools.partial(tick_kernel, offsets, turned, section),
            out_shape=shape((local_rows, model_width), BF16),
            in_specs=[VMEM] * (7 + len(flat)),
            out_specs=VMEM,
            compiler_params=params(),
            cost_estimate=cost(3 * local_rows * model_width * hidden_units, *flat),
            name="tick",
        )(grad, held, down_back, shared_gate, *scales, *flat_back)

    swap = [(i, i ^ 1) for i in range(sections)]
    for section in range(sections - 2, -1, -1):
        if section == 0:
            reduced = reduce_rows(scored, theirs, outgoing)
        if section == sections - 3:
            outgoing, scored = after((outgoing, scored))
        pairs = swap if section == sections - 2 else [(section + 1, section)]
        grad = lax.ppermute(outgoing, "section", pairs)
        if section == max(sections - 3, 0):
            theirs = swap_scored(scored)
        outgoing = tick(section, grad, outgoing)

    first, second, keep = reduced
    flips = [1 << order[-1] for order in orders(replicas)]
    terms = to_layer(first, flips[0]), to_layer(second, flips[1]), to_layer(keep, 0)
    kernel = functools.partial(finish_kernel, (local_rows * replicas) ** (-0.5))
    summed = call(kernel, "finish", [shape(keep.shape, F32)], 0, *terms)[0]
    return (outgoing[None], summed[None])


def solution(mesh):
    placed = (
        P("section", "dp", None),
        P("dp", "section"),
        P("section", "dp", None),
        P("section", "dp", None),
        P("section", None, None),
        P("section", None),
    )
    return jax.shard_map(
        on_device,
        mesh=mesh,
        in_specs=placed,
        out_specs=(P("section", "dp", None), P("section", "dp", None)),
        check_vma=False,
    )
```

```python
import functools

import jax
import jax.numpy as jnp
from jax import lax
from jax.experimental import pallas as pl
from jax.experimental.pallas import tpu as pltpu
from jax.sharding import PartitionSpec as P

F32, BF16 = jnp.float32, jnp.bfloat16
PLAIN = (((1,), (0,)), ((), ()))
TURNED = (((1,), (1,)), ((), ()))
VMEM = pl.BlockSpec(memory_space=pltpu.VMEM)
LIMIT = 16 * 2**20


def dot(left, right, dims):
    return lax.dot_general(left, right, dims, preferred_element_type=F32)


def params():
    return pltpu.CompilerParams(vmem_limit_bytes=LIMIT)


def cost(macs, *arrays):
    moved = sum(a.size * a.dtype.itemsize for a in arrays)
    return pl.CostEstimate(flops=2 * macs, bytes_accessed=moved, transcendentals=0)


def ring_place(index, size):
    return jnp.where(index % 2 == 0, index // 2, size - 1 - index // 2)


def ring_member(place, size):
    return jnp.where(place < (size + 1) // 2, 2 * place, 2 * (size - 1 - place) + 1)


def ring_pairs(size):
    order = list(range(0, size, 2)) + list(range(1, size, 2))[::-1]
    ahead = [(order[i], order[(i + 1) % size]) for i in range(size)]
    return ahead, [(b, a) for a, b in ahead]


def gather_ring(arrays, axis, between):
    size = lax.axis_size(axis)
    ahead, back = ring_pairs(size)
    pieces, offsets = [list(arrays)], [0]
    moving = [(v, v) for v in arrays]
    for step in range(1, (size - 1) // 2 + 1):
        moved = []
        for i, (v, w) in enumerate(moving):
            v, w = between(step, i, (v, w))
            both = lax.ppermute(v, axis, ahead), lax.ppermute(w, axis, back)
            moved.append(lax.optimization_barrier(both))
        moving = moved
        pieces += [[v for v, _ in moving], [w for _, w in moving]]
        offsets += [-step, step]
    if size % 2 == 0:
        (v, _), (_, w) = between(size // 2, 0, moving[0]), between(size // 2, 1, moving[1])
        pieces.append([lax.ppermute(v, axis, ahead), lax.ppermute(w, axis, back)])
        offsets.append(size // 2)
    return pieces, offsets


def gather_blocks(x, axis):
    size = lax.axis_size(axis)
    held, offsets = [x], [0]
    yield held, offsets
    for place in range(size.bit_length() - 1)[::-1]:
        stride = 1 << place
        pairs = [(i, i ^ stride) for i in range(size)]
        held += [lax.ppermute(block, axis, pairs) for block in list(held)]
        offsets += [offset ^ stride for offset in offsets]
        yield held, offsets


def after(values, *others):
    return lax.optimization_barrier((values, others))[0]


def piece_columns(offset, axis, depth):
    if offset is None:
        return slice(0, depth)
    size = lax.axis_size(axis)
    place = (ring_place(lax.axis_index(axis), size) + (offset + size)) % size
    return pl.ds(pl.multiple_of(ring_member(place, size) * depth, depth), depth)


def push_back(grad_ref, back_proj, scales, gate_vector, turned, pieces, columns, out_ref):
    gate_scale, up_scale, logit_scale = scales
    logit = jnp.sum(back_proj * logit_scale[...], axis=1, keepdims=True)
    gate_grad = (back_proj * gate_scale[...]).astype(BF16)
    up_grad = (back_proj * up_scale[...]).astype(BF16)
    for i, (where, (gate, up)) in enumerate(zip(columns, pieces)):
        dims = PLAIN if i < turned else TURNED
        through = dot(gate_grad, gate[...], dims) + dot(up_grad, up[...], dims)
        out_ref[:, where] = (
            grad_ref[:, where].astype(F32) + through + logit * gate_vector[:, where].astype(F32)
        ).astype(BF16)


def turn_kernel(*refs):
    half = len(refs) // 2
    for value, out in zip(refs[:half], refs[half:]):
        out[...] = value[...].T


def pair_up(refs):
    return [refs[i : i + 2] for i in range(0, len(refs), 2)]


def score_kernel(rows, gate_vector, score):
    logit = jnp.sum(
        rows[...].astype(F32) * gate_vector[...].astype(F32), axis=1, keepdims=True
    )
    score[...] = jax.nn.sigmoid(logit)


def prepare_kernel(offsets, down, *rest):
    blocks, (seeded, back_proj) = rest[:-2], rest[-2:]
    sections = lax.axis_size("section")
    is_last = lax.axis_index("section") == sections - 1
    width = blocks[0].shape[1]

    def lay(flip):
        for offset, block in zip(offsets, blocks):
            place = offset ^ flip
            seeded[:, place * width : (place + 1) * width] = block[...]

    pl.when(is_last)(lambda: lay(sections - 1))
    pl.when(jnp.logical_not(is_last))(lambda: lay(0))
    back_proj[...] = dot(seeded[...], down[...], TURNED)


def first_kernel(offsets, turned, rows, score, back_proj, grad, gate_vector, *rest):
    pieces, rest = pair_up(rest[: 2 * len(offsets)]), rest[2 * len(offsets) :]
    turned_pieces, rest = pair_up(rest[: 2 * turned]), rest[2 * turned :]
    out, gate_scale, up_scale, logit_scale, scored = rest
    depth = pieces[0][0].shape[0]
    columns = [piece_columns(offset, "dp", depth) for offset in offsets]
    gate_pre = up_pre = 0.0
    for where, (gate, up) in zip(columns, pieces):
        block = rows[:, where]
        gate_pre += dot(block, gate[...], PLAIN)
        up_pre += dot(block, up[...], PLAIN)
    gate_sig = jax.nn.sigmoid(gate_pre)
    activated = gate_pre * gate_sig
    hidden = (activated * up_pre).astype(BF16).astype(F32)
    share = score[...]
    gate_scale[...] = share * up_pre * gate_sig * (1.0 + gate_pre * (1.0 - gate_sig))
    up_scale[...] = share * activated
    logit_scale[...] = hidden * (share * (1.0 - share))
    scored[...] = (hidden * share).astype(BF16).T
    scales = gate_scale, up_scale, logit_scale
    section, sections = lax.axis_index("section"), lax.axis_size("section")

    @pl.when(section == sections - 1)
    def _():
        back = turned_pieces + pieces[turned:]
        push_back(grad, back_proj[...], scales, gate_vector, turned, back, columns, out)

    @pl.when(section < sections - 1)
    def _():
        out[...] = grad[...]


def tick_kernel(offsets, turned, section, grad, held, down, gate_vector, a, b, c, *rest):
    pieces, out = pair_up(rest[:-1]), rest[-1]

    here = lax.axis_index("section") == section

    @pl.when(jnp.logical_not(here))
    def _():
        out[...] = held[...]

    @pl.when(here)
    def _():
        depth = pieces[0][0].shape[1 if turned else 0]
        columns = [piece_columns(offset, "dp", depth) for offset in offsets]
        back_proj = dot(grad[...], down[...], PLAIN if turned else TURNED)
        push_back(grad, back_proj, (a, b, c), gate_vector, turned, pieces, columns, out)


def orders(size):
    top = size.bit_length() - 2
    return [0, 1, *range(top, 1, -1)], [top, 0, *range(top - 1, 0, -1)]


def own_bit(bit):
    return lax.axis_index("dp") >> bit & 1


def block_rows(order, first, second, rest, units):
    place = (first << order[0]) + (second << order[1])
    for i, bit in enumerate(order[2:]):
        place += (rest >> len(order) - 3 - i & 1) << bit
    return pl.ds(pl.multiple_of(place * units, units), units)


def split_kernel(scored, *out):
    size = lax.axis_size("dp")
    units = scored.shape[0] // size
    for order, half in zip(orders(size), out):
        for second in range(2):
            for rest in range(size // 4):
                start = (second * (size // 4) + rest) * units
                rows = block_rows(order, 1 - own_bit(order[0]), second, rest, units)
                half[start : start + units, :] = scored[rows, :]


def products_kernel(scored, grad, *rest):
    theirs, partners, sends, keeps = rest[:2], rest[2:4], rest[4:6], rest[6:]
    size = lax.axis_size("dp")
    units = scored.shape[0] // size
    half, width = sends[0].shape
    for i, order in enumerate(orders(size)):
        mine = grad[:, i * width : (i + 1) * width]

        def rows(second):
            own = own_bit(order[0])
            blocks = [
                scored[block_rows(order, own, second, rest, units), :] for rest in range(size // 4)
            ]
            where = pl.ds(pl.multiple_of(second * half, half), half)
            left = jnp.concatenate(blocks, axis=0)
            return dot(left, mine, PLAIN) + dot(theirs[i][where, :], partners[i][...], PLAIN)

        sends[i][...] = rows(1 - own_bit(order[1])).astype(BF16)
        keeps[i][...] = rows(own_bit(order[1]))


def combine_kernel(stage, *refs):
    keeps, gots, sends, kept = refs[:2], refs[2:4], refs[4:6], refs[6:]
    half, width = sends[0].shape
    for i, order in enumerate(orders(lax.axis_size("dp"))):
        own = own_bit(order[stage])

        def rows(which):
            where = pl.ds(pl.multiple_of(which * half, half), half)
            return keeps[i][where, :] + gots[i][where, :].astype(F32)

        sends[i][...] = rows(1 - own).astype(BF16)
        if len(kept) == 2:
            kept[i][...] = rows(own)
        else:
            kept[0][:, i * width : (i + 1) * width] = rows(own).astype(BF16)


def finish_kernel(factor, first, second, keep, out):
    width = first.shape[1]
    for i, got in enumerate((first, second)):
        columns = slice(i * width, (i + 1) * width)
        out[:, columns] = (got[...].astype(F32) + keep[:, columns].astype(F32)) * factor


def along(stage, values):
    size = lax.axis_size("dp")
    found = []
    for order, value in zip(orders(size), values):
        pairs = [(i, i ^ 1 << order[stage]) for i in range(size)]
        found.append(lax.ppermute(value, "dp", pairs))
    return found


def call(kernel, name, outs, macs, *args):
    return pl.pallas_call(
        kernel,
        out_shape=outs,
        in_specs=[VMEM] * len(args),
        out_specs=[VMEM] * len(outs),
        compiler_params=params(),
        cost_estimate=cost(macs, *args),
        name=name,
    )(*args)


def swap_scored(scored):
    half = jax.ShapeDtypeStruct((scored.shape[0] // 2, scored.shape[1]), BF16)
    return along(0, call(split_kernel, "split", [half] * 2, 0, scored))


def reduce_rows(scored, theirs, grad):
    stages = lax.axis_size("dp").bit_length() - 1
    rows, width = scored.shape[0] // 4, grad.shape[1]
    shape = jax.ShapeDtypeStruct
    partners = along(0, (grad[:, : width // 2], grad[:, width // 2 :]))
    half = (rows, width // 2)
    outs = [shape(half, BF16)] * 2 + [shape(half, F32)] * 2
    macs = 4 * rows * scored.shape[1] * width
    found = call(products_kernel, "products", outs, macs, scored, grad, *theirs, *partners)
    for stage in range(2, stages):
        gots = along(stage - 1, found[:2])
        rows //= 2
        half = (rows, width // 2)
        outs = [shape(half, BF16)] * 2 + [shape(half, F32)] * 2
        if stage == stages - 1:
            outs[2:] = [shape((rows, width), BF16)]
        kernel = functools.partial(combine_kernel, stage)
        found = call(kernel, "combine", outs, 0, *found[2:], *gots)
    return found


def to_layer(value, flip):
    sections, size = lax.axis_size("section"), lax.axis_size("dp")
    pairs = [
        (s * size + d, (s - 1) % sections * size + (d ^ flip))
        for s in range(sections)
        for d in range(size)
    ]
    return lax.ppermute(value, ("section", "dp"), pairs)


def on_device(stash, cotangent, gate_weight, up_weight, down_weight, shared_gate):
    sections = lax.axis_size("section")
    replicas = lax.axis_size("dp")
    local_rows, model_width = stash.shape[1:]
    depth = gate_weight.shape[1]
    down_full = down_weight[0]
    hidden_units = down_full.shape[0]

    shape = jax.ShapeDtypeStruct
    small = shape((local_rows, hidden_units), F32)
    cotangents = gather_blocks(cotangent, "section")
    blocks, block_offsets = next(cotangents)
    own_rows = stash[0]

    last_step = replicas // 2

    def between(step, i, moving):
        nonlocal blocks, own_rows
        if step == 1 and i == 0:
            mirrored = [(k, sections - 1 - k) for k in range(sections)]
            own_rows = lax.ppermute(own_rows, "section", mirrored)
        if step == 1 and i == 1:
            blocks, _ = next(cotangents, (blocks, None))
        if step == 2 and i == 0:
            moving, blocks = after((moving, blocks))
        if step == last_step - 1 and i == 0:
            blocks, _ = next(cotangents, (list(blocks), None))
        if step == last_step - 1 and i == 1:
            moving, own_rows = after((moving, own_rows))
        if step == last_step and i == 0:
            moving, blocks = after((moving, blocks))
        return moving

    pieces, offsets = gather_ring([gate_weight[0], up_weight[0]], "dp", between)
    for blocks, _ in cotangents:
        pass
    turned = 0 if depth % 128 else len(pieces)
    down_back = down_full
    if turned:
        outs = [shape(down_full.shape[::-1], BF16)]
        down_back = call(turn_kernel, "turn_down", outs, 0, down_full)[0]
    outs = [shape((hidden_units, depth), BF16)] * 2
    turned_pieces = [call(turn_kernel, "turn", outs, 0, *piece) for piece in pieces[:turned]]
    seeded, back_proj = pl.pallas_call(
        functools.partial(prepare_kernel, block_offsets),
        out_shape=[shape((local_rows, model_width), BF16), small],
        in_specs=[VMEM] * (1 + len(blocks)),
        out_specs=[VMEM] * 2,
        compiler_params=params(),
        cost_estimate=cost(local_rows * model_width * hidden_units, down_full),
        name="prepare",
    )(down_full, *blocks)
    score = pl.pallas_call(
        score_kernel,
        out_shape=shape((local_rows, 1), F32),
        in_specs=[VMEM] * 2,
        out_specs=VMEM,
        compiler_params=params(),
        cost_estimate=cost(local_rows * model_width, own_rows),
        name="score",
    )(own_rows, shared_gate)

    if depth % 128:
        size = replicas
        place = ring_place(lax.axis_index("dp"), size)
        joined = [jnp.zeros((depth * replicas, hidden_units), BF16)] * 2
        for offset, piece in zip(offsets, pieces):
            start = ring_member((place + offset + size) % size, size) * depth
            joined = [lax.dynamic_update_slice(j, p, (start, 0)) for j, p in zip(joined, piece)]
        pieces, offsets = [joined], [None]
    flat = [v for piece in pieces for v in piece]
    flat_turned = [v for piece in turned_pieces for v in piece]
    flat_back = flat_turned + flat[2 * turned :]

    outgoing, *scales, scored = pl.pallas_call(
        functools.partial(first_kernel, offsets, turned),
        out_shape=[
            shape((local_rows, model_width), BF16),
            small,
            small,
            small,
            shape((hidden_units, local_rows), BF16),
        ],
        in_specs=[VMEM] * (5 + len(flat) + 2 * turned),
        out_specs=[VMEM] * 5,
        compiler_params=params(),
        cost_estimate=cost(4 * local_rows * model_width * hidden_units, *flat),
        name="first_tick",
    )(own_rows, score, back_proj, seeded, shared_gate, *flat, *flat_turned)
    around = [(i, (i + 1) % sections) for i in range(sections)]
    scored = lax.ppermute(scored, "section", around)

    def tick(section, grad, held):
        return pl.pallas_call(
            functools.partial(tick_kernel, offsets, turned, section),
            out_shape=shape((local_rows, model_width), BF16),
            in_specs=[VMEM] * (7 + len(flat)),
            out_specs=VMEM,
            compiler_params=params(),
            cost_estimate=cost(3 * local_rows * model_width * hidden_units, *flat),
            name="tick",
        )(grad, held, down_back, shared_gate, *scales, *flat_back)

    swap = [(i, i ^ 1) for i in range(sections)]
    for section in range(sections - 2, -1, -1):
        if section == 0:
            reduced = reduce_rows(scored, theirs, outgoing)
        if section == sections - 3:
            outgoing, scored = after((outgoing, scored))
        pairs = swap if section == sections - 2 else [(section + 1, section)]
        grad = lax.ppermute(outgoing, "section", pairs)
        if section == max(sections - 3, 0):
            theirs = swap_scored(scored)
        outgoing = tick(section, grad, outgoing)

    first, second, keep = reduced
    flips = [1 << order[-1] for order in orders(replicas)]
    terms = to_layer(first, flips[0]), to_layer(second, flips[1]), to_layer(keep, 0)
    kernel = functools.partial(finish_kernel, (local_rows * replicas) ** (-0.5))
    summed = call(kernel, "finish", [shape(keep.shape, F32)], 0, *terms)[0]
    return (outgoing[None], summed[None])


def solution(mesh):
    placed = (
        P("section", "dp", None),
        P("dp", "section"),
        P("section", "dp", None),
        P("section", "dp", None),
        P("section", None, None),
        P("section", None),
    )
    return jax.shard_map(
        on_device,
        mesh=mesh,
        in_specs=placed,
        out_specs=(P("section", "dp", None), P("section", "dp", None)),
        check_vma=False,
    )
```
